256 devices in a mesh: phase: 4 (over x), ctx: 64 (over z, y, core).
Axes of the slice: x: 4, y: 4, z: 8, core: 2. Of those that a mesh axis runs over, the one named last changes fastest.
Arguments:
- tokens: bfloat16 [1, 8192, 4096], P(None, 'ctx', 'phase'), may hold values from -6 to 6
- queries: bfloat16 [4, 1, 8192, 4096], P('phase', None, 'ctx'), may hold values from -2 to 2
- keys_in: bfloat16 [4, 1, 8192, 4096], P('phase', None, 'ctx'), may hold values from -2 to 2
- values: bfloat16 [4, 1, 8192, 4096], P('phase', None, 'ctx'), may hold values from -6 to 6
- norm_gain: bfloat16 [4, 4096], P('phase'), may hold values from 0.5 to 1.5
- log_decay: float32 [4, 1, 32, 8192], P('phase', None, None, 'ctx'), may hold values from -1.2 to 0, as said below
- doc_ids: int32 [1, 8192], P(None, 'ctx'), may hold values from 0 to 7, never falling along the last dimension, each value on 1 to 4096 neighbouring positions
Outputs:
- phase_out: bfloat16 [4, 1, 8192, 4096], P('phase', None, 'ctx')
The draws below stay inside these ranges and needn't reach their ends.
Inputs may be any that keep to these rules, and one draw needn't show every extreme that they name: `log_decay`: each entry is the log of one position's decay factor for one head.
All inputs are finite; a program needn't handle non-finite values.
Results may differ from the reference program's by a relative error of at most 0.006.
Values may be sent and summed in bfloat16 or wider, within the bound.
No kernel may reach another device: no remote copies, remote signals or barrier semaphores. Data moves between devices by JAX's collectives and lax.ppermute only.
A program may use at most 320 MiB of HBM per device.

```python
import math
import jax
import jax.numpy as jnp
import numpy as np
from jax import lax

HEADS = 32
HEAD = 128
TOK_DEV = 128
MICRO = 1
DOCS = 8
PHASES = 4
CHANNELS = 4096
TOKENS = 8192


def draw_log_decay(key, part):
    keys_list = jax.random.split(key, 6)
    groups = PHASES * MICRO
    orders = jax.vmap(lambda single: jax.random.permutation(single, HEADS))(jax.random.split(keys_list[0], groups))
    orders = orders.reshape(PHASES, MICRO, HEADS)
    fast = orders < HEADS // 2
    fast_rate = jnp.exp(jax.random.uniform(keys_list[1], (PHASES, MICRO, HEADS), jnp.float32, math.log(1.0 / 50.0), math.log(1.0 / 30.0)))
    slow_rate = jax.random.uniform(keys_list[2], (PHASES, MICRO, HEADS), jnp.float32, 0.25, 1.0) / TOKENS
    fading_speed = jnp.where(fast, fast_rate, slow_rate)
    approximate_guess = jnp.exp(jax.random.uniform(keys_list[3], (PHASES, MICRO, HEADS, TOKENS), jnp.float32, -math.log(2.0), math.log(2.0)))
    segment_start_marks = jax.random.randint(keys_list[4], (PHASES, MICRO, HEADS, 2), 0, TOKENS)
    fading_falloffs = jnp.log(jax.random.uniform(keys_list[5], (PHASES, MICRO, HEADS, 2), jnp.float32, 0.6, 0.85))
    restart_indices = jnp.arange(TOKENS)
    tile_span_count = jnp.sum(jnp.where(restart_indices[None, None, None, None, :] == segment_start_marks[..., None], fading_falloffs[..., None], 0.0), axis=3)
    return (-fading_speed[..., None] * approximate_guess + tile_span_count).astype(jnp.float32)


def block_scale(rng, shape, cuts, least, top_value):
    def one(axis_at, parts):
        steps = jax.random.uniform(jax.random.fold_in(jax.random.fold_in(rng, 6), axis_at), (parts,), jnp.float32, least / len(cuts), top_value / len(cuts))
        return jnp.repeat(jnp.exp(steps), shape[axis_at] // parts).reshape((-1,) + (1,) * (len(shape) - axis_at - 1))

    level = one(*cuts[0])
    for cut in cuts[1:]:
        level = level * one(*cut)
    return level


def length_profile(number_of, total, limit, skew):
    portions = [(1 << 20) // math.isqrt(grade ** skew) + 1 for grade in range(2, number_of + 1)]
    surplus, given = total - limit - (number_of - 1), [1] * (number_of - 1)
    while surplus > 0:
        candidates = [i for i in range(number_of - 1) if given[i] < limit]
        whole, remaining = sum([portions[i] for i in candidates]), surplus
        for i in candidates:
            addition = min(limit - given[i], max(1, remaining * portions[i] // whole), surplus)
            given[i] = given[i] + addition
            surplus = surplus - addition
    return np.array([limit] + given)


def ragged(key, number_of, total, most, lean):
    if number_of == 2:
        one = jax.random.randint(key, (), max(1, total - most), min(most, total - 1) + 1)
        return jnp.stack([one, total - one])
    lengths = jnp.asarray(length_profile(number_of, total, most, lean), jnp.int32)
    twos = (number_of - 1) // 2
    source_of, receiver = lengths[1:1 + 2 * twos:2], lengths[2:2 + 2 * twos:2]
    room = jnp.minimum(source_of - 1, most - receiver)
    moved = jax.random.randint(jax.random.fold_in(key, 1), (twos,), 0, 1 << 20) % (room + 1)
    lengths = lengths.at[1:1 + 2 * twos:2].set(source_of - moved).at[2:2 + 2 * twos:2].set(receiver + moved)
    return lengths[jax.random.permutation(jax.random.fold_in(key, 2), number_of)]


def centred(rng, shape, scale, most, cuts=(), kind=jnp.bfloat16):
    level = block_scale(rng, shape, cuts, -0.22, 0.18) if cuts else 1.0
    values = jax.random.normal(rng, shape, jnp.float32) * scale * level
    return jnp.minimum(jnp.maximum(values, -most), most).astype(kind)


def setup_inputs(seed: int = 0) -> dict:
    splits = jax.random.split(jax.random.key(seed), 8)
    tokens = centred(splits[0], (MICRO, TOKENS, CHANNELS), 1.0, 6.0, ((1, 64), (2, 4)))
    queries = centred(splits[1], (PHASES, MICRO, TOKENS, CHANNELS), 0.3, 2.0, ((0, 4), (2, 64)))
    keys_in = centred(splits[2], (PHASES, MICRO, TOKENS, CHANNELS), 0.3, 2.0, ((0, 4), (2, 64)))
    values = centred(splits[3], (PHASES, MICRO, TOKENS, CHANNELS), 1.0, 6.0, ((0, 4), (2, 64)))
    norm_gain = jnp.clip(1.0 + 0.1 * jax.random.normal(splits[4], (PHASES, CHANNELS), jnp.float32), 0.5, 1.5).astype(jnp.bfloat16)
    log_decay = draw_log_decay(jax.random.fold_in(splits[7], 71), 0)
    doc_ids = jax.vmap(lambda own: jnp.searchsorted(jnp.cumsum(ragged(own, DOCS, TOKENS, TOKENS // 2, 1)), jnp.arange(TOKENS), side="right"))(jax.random.split(splits[6], MICRO)).reshape((MICRO, TOKENS)).astype(jnp.int32)
    return dict(tokens=tokens, queries=queries, keys_in=keys_in, values=values, norm_gain=norm_gain, log_decay=log_decay, doc_ids=doc_ids)


EPSILON = 1e-05

def local_terms(queries, keys_all, values, block_decay, block_document_ids):
    decay_sum = jnp.cumsum(block_decay, axis=1)
    length = block_document_ids.shape[0]
    steps = jnp.arange(length)
    allowed = (steps[None, :] <= steps[:, None]) & (block_document_ids[None, :] == block_document_ids[:, None])
    spread = decay_sum[:, :, None] - decay_sum[:, None, :]
    weighting = jnp.where(allowed[None], jnp.exp(jnp.minimum(spread, 0.0)), 0.0)
    scores = jnp.einsum('thd,shd->hts', queries.astype(jnp.float32), keys_all.astype(jnp.float32))
    attn = lax.optimization_barrier((scores * weighting).astype(jnp.bfloat16))
    intra = jnp.einsum('hts,shd->thd', attn.astype(jnp.float32), values.astype(jnp.float32))
    same_doc = (block_document_ids == block_document_ids[-1]).astype(jnp.float32)
    carried = jnp.exp(decay_sum[:, -1:] - decay_sum) * same_doc[None, :]
    keyed = lax.optimization_barrier((keys_all.astype(jnp.float32) * carried.T[:, :, None]).astype(jnp.bfloat16))
    summary = jnp.einsum('thi,thj->hij', keyed.astype(jnp.float32), values.astype(jnp.float32))
    factor = jnp.exp(decay_sum[:, -1]) * (block_document_ids[0] == block_document_ids[-1]).astype(jnp.float32)
    return (decay_sum, intra, summary, factor)

def finish(block_in, queries, decay_sum, intra, prefix, block_document_ids, gain):
    length = block_in.shape[0]
    leading = (block_document_ids == block_document_ids[0]).astype(jnp.float32)
    rounded = lax.optimization_barrier(prefix.astype(jnp.bfloat16))
    inter = jnp.einsum('thi,hij->thj', queries.astype(jnp.float32), rounded.astype(jnp.float32))
    scaling = jnp.exp(decay_sum).T * leading[:, None]
    total = intra + inter * scaling[:, :, None]
    power = lax.optimization_barrier(jnp.mean(total * total, axis=-1, keepdims=True))
    normed = total * lax.rsqrt(power + EPSILON) * gain.reshape(HEADS, HEAD).astype(jnp.float32)
    return (block_in.astype(jnp.float32) + normed.reshape(length, HEADS * HEAD)).astype(jnp.bfloat16)

def layer(layer_in, query_rows, key_rows, value_rows, gain, decay_rows, docs):
    blocks = TOKENS // TOK_DEV
    in_blocks = layer_in.reshape(blocks, TOK_DEV, HEADS * HEAD)
    asking_tiles = query_rows.reshape(blocks, TOK_DEV, HEADS, HEAD)
    key_blocks = key_rows.reshape(blocks, TOK_DEV, HEADS, HEAD)
    value_blocks = value_rows.reshape(blocks, TOK_DEV, HEADS, HEAD)
    decay_blocks = decay_rows.reshape(HEADS, blocks, TOK_DEV).transpose(1, 0, 2)
    doc_blocks = docs.reshape(blocks, TOK_DEV)

    def advance(carry, block):
        state, last_doc = carry
        block_in, block_q, block_k, block_v, block_decay, block_document_ids = block
        decay_sum, intra, summary, factor = local_terms(block_q, block_k, block_v, block_decay, block_document_ids)
        prefix = state * (last_doc == block_document_ids[0]).astype(jnp.float32)
        result = finish(block_in, block_q, decay_sum, intra, prefix, block_document_ids, gain)
        return ((factor[:, None, None] * prefix + summary, block_document_ids[-1]), result)
    start = (jnp.zeros((HEADS, HEAD, HEAD), jnp.float32), jnp.array(-1, jnp.int32))
    closing, results = lax.scan(advance, start, (in_blocks, asking_tiles, key_blocks, value_blocks, decay_blocks, doc_blocks))
    return results.reshape(TOKENS, HEADS * HEAD)

def reference(tokens, queries, keys_in, values, norm_gain, log_decay, doc_ids):
    outputs = []
    for phase_pos in range(PHASES):
        row_list = []
        for micro_pos in range(MICRO):
            if phase_pos == 0:
                layer_in = tokens[micro_pos]
            else:
                layer_in = outputs[phase_pos - 1][micro_pos]
            row_list.append(layer(layer_in, queries[phase_pos, micro_pos], keys_in[phase_pos, micro_pos], values[phase_pos, micro_pos], norm_gain[phase_pos], log_decay[phase_pos, micro_pos], doc_ids[micro_pos]))
        outputs.append(row_list)
    return jnp.stack([jnp.stack(row_list) for row_list in outputs])
```

```python
import functools

import jax
import jax.numpy as jnp
from jax import lax
from jax.experimental import pallas as pl
from jax.experimental.pallas import tpu as pltpu
from jax.sharding import Mesh
from jax.sharding import PartitionSpec as P

EPSILON = 1e-05
F32, BF16 = jnp.float32, jnp.bfloat16
D = 128
HEADS = 32
HALF = HEADS // 2
GROUP = HALF // 4
NZ = 8
META = 32
ROWS = GROUP * D
PART = ROWS + META
HIGHEST = lax.Precision.HIGHEST
VMEM_LIMIT = 40 * 1024 * 1024


def nt(a, b, precision=None):
    return lax.dot_general(a, b, (((1,), (1,)), ((), ())), precision=precision, preferred_element_type=F32)


def tn(a, b):
    return lax.dot_general(a, b, (((0,), (0,)), ((), ())), preferred_element_type=F32)


def iota(shape, axis):
    return lax.broadcasted_iota(jnp.int32, shape, axis)


def lower():
    return (iota((D, D), 1) <= iota((D, D), 0)).astype(F32)


def rows_of(ids_row):
    return jnp.transpose(jnp.broadcast_to(ids_row, (D, D)))


def split3(x):
    hi = x.astype(BF16).astype(F32)
    mid = (x - hi).astype(BF16).astype(F32)
    return hi, mid, x - hi - mid


def pack_meta(decay, first, last):
    row = iota((8, D), 0)
    ids = jnp.where(row == 0, first, jnp.where(row == 1, last, 0.0))
    return jnp.concatenate([*split3(decay), ids], axis=0).astype(BF16)


def unpack_meta(meta):
    meta = meta.astype(F32)
    return meta[0:8] + meta[8:16] + meta[16:24], meta[24:25], meta[25:26]


def same(a, b):
    return (a == b).astype(F32)


def summary_kernel(index, k_ref, v_ref, decay_ref, ids_ref, out_ref, cut_ref):
    half = index[0]
    ids = ids_ref[...].astype(F32)
    first, last = ids[:, 0:1], ids[:, D - 1 : D]
    decay = decay_ref[pl.ds(pl.multiple_of(half * HALF, HALF), HALF), :]
    sums = nt(lower(), decay, HIGHEST)
    column = same(rows_of(ids)[:, 0:HALF], last)
    carried = jnp.exp(sums[D - 1 : D, :] - sums) * column
    total = lax.dot_general(
        decay, jnp.ones((D, D), F32), (((1,), (0,)), ((), ())), precision=HIGHEST, preferred_element_type=F32
    )
    for group in range(4):
        for i in range(GROUP):
            h = group * GROUP + i
            lanes = slice(h * D, (h + 1) * D)
            keyed = (k_ref[:, lanes].astype(F32) * carried[:, h : h + 1]).astype(BF16)
            out_ref[group, i * D : (i + 1) * D, :] = tn(keyed, v_ref[:, lanes]).astype(BF16)
        cut_ref[0:GROUP, :] = total[group * GROUP : (group + 1) * GROUP, :]
        cut_ref[GROUP:8, :] = jnp.zeros((8 - GROUP, D), F32)
        out_ref[group, ROWS:PART, :] = pack_meta(
            cut_ref[...], jnp.broadcast_to(first, (1, D)), jnp.broadcast_to(last, (1, D))
        )


def summaries(half, keys, values, decay, ids):
    whole = lambda shape: pl.BlockSpec(shape, lambda i, s: (0,) * len(shape))
    return pl.pallas_call(
        summary_kernel,
        out_shape=jax.ShapeDtypeStruct((4, PART, D), BF16),
        grid_spec=pltpu.PrefetchScalarGridSpec(
            num_scalar_prefetch=1,
            grid=(1,),
            in_specs=[
                pl.BlockSpec((D, HALF * D), lambda i, s: (0, s[0])),
                pl.BlockSpec((D, HALF * D), lambda i, s: (0, s[0])),
                whole((HEADS, D)),
                whole((1, D)),
            ],
            out_specs=whole((4, PART, D)),
            scratch_shapes=[pltpu.VMEM((8, D), F32)],
        ),
        compiler_params=pltpu.CompilerParams(vmem_limit_bytes=VMEM_LIMIT),
        cost_estimate=pl.CostEstimate(flops=2 * HALF * D**3, bytes_accessed=3 * HALF * D * D * 2, transcendentals=0),
    )(half, keys, values, decay, ids)


def intra_kernel(q_ref, k_ref, v_ref, decay_ref, ids_ref, out_ref):
    ids = ids_ref[...].astype(F32)
    heads = q_ref.shape[1] // D
    decay = decay_ref[...]
    sums_column = nt(lower(), decay, HIGHEST)
    sums_row = nt(decay, lower(), HIGHEST)
    allowed = (iota((D, D), 1) <= iota((D, D), 0)) & (rows_of(ids) == ids)
    for h in range(heads):
        lanes = slice(h * D, (h + 1) * D)
        spread = jnp.minimum(sums_column[:, h : h + 1] - sums_row[h : h + 1, :], 0.0)
        weighting = jnp.where(allowed, jnp.exp(spread), 0.0)
        attn = (nt(q_ref[:, lanes], k_ref[:, lanes]) * weighting).astype(BF16)
        out_ref[:, lanes] = jnp.dot(attn, v_ref[:, lanes], preferred_element_type=F32)


def intra_term(queries, keys, values, decay, ids):
    step = 8
    block = pl.BlockSpec((D, step * D), lambda i: (0, i))
    return pl.pallas_call(
        intra_kernel,
        out_shape=jax.ShapeDtypeStruct((D, HEADS * D), F32),
        grid=(HEADS // step,),
        in_specs=[block, block, block, pl.BlockSpec((step, D), lambda i: (i, 0)), pl.BlockSpec((1, D), lambda i: (0, 0))],
        out_specs=block,
        compiler_params=pltpu.CompilerParams(vmem_limit_bytes=VMEM_LIMIT),
        cost_estimate=pl.CostEstimate(
            flops=4 * HEADS * D**3, bytes_accessed=5 * HEADS * D * D * 2, transcendentals=HEADS * D * D
        ),
    )(queries, keys, values, decay, ids)


def chip_kernel(index, own_ref, other_ref, *out_refs):
    y, core = index[0], index[1]
    is_one = core == 1
    for step in range(4):
        group = lax.rem(y + step, 4)
        decay_own, first_own, last_own = unpack_meta(own_ref[group, ROWS:PART, :])
        decay_other, first_other, last_other = unpack_meta(other_ref[group, ROWS:PART, :])
        joined = same(last_own, last_other)
        later = jnp.where(is_one, decay_own, decay_other)
        passed = jnp.exp(later) * joined
        weight_own = jnp.where(is_one, 1.0, passed)
        weight_other = jnp.where(is_one, passed, 1.0)
        for i in range(GROUP):
            rows = slice(i * D, (i + 1) * D)
            out_refs[step][rows, :] = (
                weight_own[i : i + 1] * own_ref[group, rows, :].astype(F32)
                + weight_other[i : i + 1] * other_ref[group, rows, :].astype(F32)
            ).astype(BF16)
        out_refs[step][ROWS:PART, :] = pack_meta(
            decay_own + decay_other,
            jnp.where(is_one, first_other, first_own),
            jnp.where(is_one, last_own, last_other),
        )


def small_call(kernel, index, operands, outs, scratch=()):
    whole = lambda shape: pl.BlockSpec(shape, lambda i, s: (0,) * len(shape))
    size = sum(a.size * a.dtype.itemsize for a in operands)
    return pl.pallas_call(
        kernel,
        out_shape=[jax.ShapeDtypeStruct(shape, dtype) for shape, dtype in outs],
        grid_spec=pltpu.PrefetchScalarGridSpec(
            num_scalar_prefetch=1,
            grid=(1,),
            in_specs=[whole(a.shape) for a in operands],
            out_specs=[whole(shape) for shape, _ in outs],
            scratch_shapes=list(scratch),
        ),
        compiler_params=pltpu.CompilerParams(vmem_limit_bytes=VMEM_LIMIT),
        cost_estimate=pl.CostEstimate(flops=size, bytes_accessed=2 * size, transcendentals=0),
    )(index, *operands)


def in_order(y, slots, ordered_ref):
    for step in range(4):
        ordered_ref[lax.rem(y + 4 - step, 4)] = slots[step][...]


def row_kernel(index, *refs):
    *slots, out_ref, ordered_ref = refs
    in_order(index[0], slots, ordered_ref)
    metas = [unpack_meta(ordered_ref[c, ROWS:PART, :]) for c in range(4)]
    weights, after = [None] * 4, jnp.zeros((8, D), F32)
    for c in (3, 2, 1, 0):
        weights[c] = jnp.exp(after) * same(metas[c][2], metas[3][2])
        after = after + metas[c][0]
    row = iota((16, D), 0)
    for i in range(GROUP):
        rows = slice(i * D, (i + 1) * D)
        state = sum(weights[c][i : i + 1] * ordered_ref[c, rows, :].astype(F32) for c in range(4)).astype(BF16)
        out_ref[2 * i, 0 : D // 2, :] = state[0 : D // 2]
        out_ref[2 * i + 1, 0 : D // 2, :] = state[D // 2 :]
        hi, mid, low = split3(after[i : i + 1])
        meta = jnp.zeros((16, D), F32)
        for at, value in enumerate((hi, mid, low, metas[0][1], metas[3][2])):
            meta = jnp.where(row == at, value, meta)
        out_ref[2 * i, D // 2 :, :] = meta.astype(BF16)
        out_ref[2 * i + 1, D // 2 :, :] = meta.astype(BF16)


def scan_kernel(index, in_ref, out_ref):
    del index
    state = jnp.zeros((D // 2, D), F32)
    before = jnp.full((1, D), -1.0, F32)
    for z in range(NZ):
        meta = in_ref[z, D // 2 :, :].astype(F32)
        decay, first, last = meta[0:1] + meta[1:2] + meta[2:3], meta[3:4], meta[4:5]
        state = state * same(before, first)
        out_ref[z] = state.astype(BF16)
        state = jnp.exp(decay) * same(first, last) * state + in_ref[z, 0 : D // 2, :].astype(F32)
        before = last


def spread_kernel(index, state_ref, *refs):
    *slots, out0, out1, out2, out3, ordered_ref, result_ref = refs
    y = index[0]
    in_order(y, slots, ordered_ref)
    metas = [unpack_meta(ordered_ref[c, ROWS:PART, :]) for c in range(4)]
    passing = [jnp.exp(decay) * same(first, last) for decay, first, last in metas]
    joined = [None] + [same(metas[c - 1][2], metas[c][1]) for c in (1, 2, 3)]
    for i in range(GROUP):
        rows = slice(i * D, (i + 1) * D)
        state = state_ref[rows, :].astype(F32)
        result_ref[0, rows, :] = state.astype(BF16)
        for c in (1, 2, 3):
            state = passing[c - 1][i : i + 1] * state + ordered_ref[c - 1, rows, :].astype(F32)
            state = state * joined[c]
            result_ref[c, rows, :] = state.astype(BF16)
    for step, out_ref in enumerate((out0, out1, out2, out3)):
        out_ref[...] = result_ref[lax.rem(y + step, 4)]


def core_kernel(index, own_ref, other_ref, s0, s1, s2, s3, mine_ref, send_ref):
    y, core = index[0], index[1]
    is_one = core == 1
    for step, slot in enumerate((s0, s1, s2, s3)):
        group = lax.rem(y + 4 - step, 4)
        decay_own, first_own, last_own = unpack_meta(own_ref[group, ROWS:PART, :])
        decay_other, first_other, last_other = unpack_meta(other_ref[group, ROWS:PART, :])
        decay = jnp.where(is_one, decay_other, decay_own)
        first0 = jnp.where(is_one, first_other, first_own)
        last0 = jnp.where(is_one, last_other, last_own)
        first1 = jnp.where(is_one, first_own, first_other)
        joined = same(last0, first1)
        passing = jnp.exp(decay) * same(first0, last0) * joined
        for i in range(GROUP):
            rows = slice(i * D, (i + 1) * D)
            chip = slot[rows, :]
            earlier = jnp.where(is_one, other_ref[group, rows, :].astype(F32), own_ref[group, rows, :].astype(F32))
            later = (passing[i : i + 1] * chip.astype(F32) + joined * earlier).astype(BF16)
            mine_ref[group, rows, :] = jnp.where(is_one, later.astype(F32), chip.astype(F32)).astype(BF16)
            send_ref[group, rows, :] = jnp.where(is_one, chip.astype(F32), later.astype(F32)).astype(BF16)


def attend_kernel(index, q_ref, intra_ref, mine_ref, other_ref, decay_ref, ids_ref, gain_ref, *out_refs):
    step = pl.program_id(0)
    quarter = lax.rem(index[0] + step, 4)
    use_mine = (quarter // 2) == index[1]
    ids = ids_ref[...].astype(F32)
    decay = decay_ref[...]
    sums = nt(lower(), decay, HIGHEST)
    scaling = jnp.exp(sums) * same(rows_of(ids)[:, 0:8], ids[:, 0:1])
    for i in range(8):
        lanes = slice(i * D, (i + 1) * D)
        rows = slice((i % GROUP) * D, (i % GROUP + 1) * D)
        mine, other = mine_ref[i // GROUP, rows, :], other_ref[i // GROUP, rows, :]
        state = jnp.where(use_mine, mine.astype(F32), other.astype(F32)).astype(BF16)
        inter = jnp.dot(q_ref[:, lanes], state, preferred_element_type=F32)
        total = intra_ref[:, lanes] + inter * scaling[:, i : i + 1]
        power = jnp.sum(total * total, axis=1, keepdims=True) * (1.0 / D)
        normed = (total * lax.rsqrt(power + EPSILON) * gain_ref[:, lanes].astype(F32)).astype(BF16)
        for at, out_ref in enumerate(out_refs):

            @pl.when(step == at)
            def _(out_ref=out_ref, normed=normed, lanes=lanes):
                out_ref[:, lanes] = normed


def attend(index, queries, intra, mine, other, decay, ids, gain):
    quarter = lambda i, s: lax.rem(s[0] + i, 4)
    block = pl.BlockSpec((D, 8 * D), lambda i, s: (0, quarter(i, s)))
    states = pl.BlockSpec((2, ROWS, D), lambda i, s: (lax.rem(quarter(i, s), 2), 0, 0))
    return pl.pallas_call(
        attend_kernel,
        out_shape=[jax.ShapeDtypeStruct((D, 8 * D), BF16)] * 4,
        grid_spec=pltpu.PrefetchScalarGridSpec(
            num_scalar_prefetch=1,
            grid=(4,),
            in_specs=[
                block,
                block,
                states,
                states,
                pl.BlockSpec((8, D), lambda i, s: (quarter(i, s), 0)),
                pl.BlockSpec((1, D), lambda i, s: (0, 0)),
                pl.BlockSpec((1, 8 * D), lambda i, s: (0, quarter(i, s))),
            ],
            out_specs=[pl.BlockSpec((D, 8 * D), lambda i, s: (0, 0))] * 4,
        ),
        compiler_params=pltpu.CompilerParams(vmem_limit_bytes=VMEM_LIMIT),
        cost_estimate=pl.CostEstimate(
            flops=2 * HEADS * D**3, bytes_accessed=7 * HEADS * D * D * 2, transcendentals=HEADS * D
        ),
    )(index, queries, intra, mine, other, decay, ids, gain)


def layers_kernel(index, tokens_ref, *refs):
    *slots, out0, out1, out2, out3, ordered_ref = refs
    phase = index[0]
    in_order(phase, slots, ordered_ref)
    current = tokens_ref[...].astype(F32)
    for s in range(4):
        rounded = (current + ordered_ref[s].astype(F32)).astype(BF16)
        ordered_ref[s] = rounded
        current = rounded.astype(F32)
    for step, out_ref in enumerate((out0, out1, out2, out3)):
        out_ref[...] = ordered_ref[lax.rem(phase + step, 4)]


def place_kernel(index, *refs):
    *slots, out_ref = refs
    quarter = pl.program_id(0)
    source = lax.rem(index[0] + 4 - quarter, 4)
    for step, slot in enumerate(slots):

        @pl.when(source == step)
        def _(slot=slot):
            out_ref[...] = slot[...]


def place(index, slots):
    return pl.pallas_call(
        place_kernel,
        out_shape=jax.ShapeDtypeStruct((D, HEADS * D), BF16),
        grid_spec=pltpu.PrefetchScalarGridSpec(
            num_scalar_prefetch=1,
            grid=(4,),
            in_specs=[pl.BlockSpec((D, 8 * D), lambda i, s: (0, 0))] * 4,
            out_specs=pl.BlockSpec((D, 8 * D), lambda i, s: (0, i)),
        ),
        compiler_params=pltpu.CompilerParams(vmem_limit_bytes=VMEM_LIMIT),
        cost_estimate=pl.CostEstimate(flops=0, bytes_accessed=4 * HEADS * D * D, transcendentals=0),
    )(index, *slots)


def ring_exchange(slots, axis):
    size = lax.axis_size(axis)
    moved = [
        lax.ppermute(slots[d], axis, [(i, (i + d) % size) for i in range(size)]) for d in range(1, len(slots))
    ]
    return [slots[0], *moved]


def swap_cores(array):
    return lax.ppermute(array, "core", [(0, 1), (1, 0)])


def local(tokens, queries, keys_in, values, norm_gain, log_decay, doc_ids):
    phase, y, core = (lax.axis_index(name) for name in ("phase", "y", "core"))
    queries, keys, values, decay = queries[0, 0], keys_in[0, 0], values[0, 0], log_decay[0, 0]
    here = jnp.stack([y, core]).astype(jnp.int32)

    sending = summaries(jnp.stack([1 - core]), keys, values, decay, doc_ids)
    other = swap_cores(sending)
    own = summaries(jnp.stack([core]), keys, values, decay, doc_ids)

    group_out = ((PART, D), BF16)
    slots = ring_exchange(small_call(chip_kernel, here, [own, other], [group_out] * 4), "y")
    intra = intra_term(queries, keys, values, decay, doc_ids)

    (pieces,) = small_call(
        row_kernel, here, slots, [((NZ, D // 2 + 16, D), BF16)], [pltpu.VMEM((4, PART, D), BF16)]
    )
    pieces = lax.all_to_all(pieces, "z", split_axis=0, concat_axis=0, tiled=True)
    (states,) = small_call(scan_kernel, here, [pieces], [((NZ, D // 2, D), BF16)])
    states = lax.all_to_all(states, "z", split_axis=0, concat_axis=0, tiled=True)

    spread = small_call(
        spread_kernel,
        here,
        [states.reshape(ROWS, D), *slots],
        [((ROWS, D), BF16)] * 4,
        [pltpu.VMEM((4, PART, D), BF16), pltpu.VMEM((4, ROWS, D), BF16)],
    )
    spread = ring_exchange(spread, "y")
    mine, send = small_call(core_kernel, here, [own, other, *spread], [((4, ROWS, D), BF16)] * 2)
    theirs = swap_cores(send)

    at = jnp.stack([phase, core]).astype(jnp.int32)
    normed = ring_exchange(attend(at, queries, intra, mine, theirs, decay, doc_ids, norm_gain), "phase")
    quarter_out = ((D, 8 * D), BF16)
    sums = small_call(
        layers_kernel, at, [tokens[0], *normed], [quarter_out] * 4, [pltpu.VMEM((4, D, 8 * D), BF16)]
    )
    return place(at, ring_exchange(sums, "phase"))[None, None]


def solution(mesh):
    grid = Mesh(mesh.devices.reshape(4, NZ, 4, 2), ("phase", "z", "y", "core"))
    ctx = ("z", "y", "core")
    rows = P("phase", None, ctx, None)
    return jax.shard_map(
        local,
        mesh=grid,
        in_specs=(
            P(None, ctx, "phase"),
            rows,
            rows,
            rows,
            P("phase", None),
            P("phase", None, None, ctx),
            P(None, ctx),
        ),
        out_specs=rows,
        check_vma=False,
    )
```

```python
import functools

import jax
import jax.numpy as jnp
from jax import lax
from jax.experimental import pallas as pl
from jax.experimental.pallas import tpu as pltpu
from jax.sharding import Mesh
from jax.sharding import PartitionSpec as P

EPSILON = 1e-05
F32, BF16 = jnp.float32, jnp.bfloat16
D = 128
HEADS = 32
HALF = HEADS // 2
GROUP = HALF // 4
NZ = 8
META = 32
ROWS = GROUP * D
PART = ROWS + META
VMEM_LIMIT = 16 * 1024 * 1024
ATTEND_LIMIT = 52 * 1024 * 1024
INTRA_LIMIT = 60 * 1024 * 1024


def nt(a, b):
    return lax.dot_general(a, b, (((1,), (1,)), ((), ())), preferred_element_type=F32)


def iota(shape, axis):
    return lax.broadcasted_iota(jnp.int32, shape, axis)


def split3(x):
    hi = x.astype(BF16).astype(F32)
    mid = (x - hi).astype(BF16).astype(F32)
    return hi, mid, x - hi - mid


def three_parts(x):
    return jnp.concatenate([part.astype(BF16) for part in split3(x)], axis=1)


def running_sums(decay):
    shape = (D, 3 * D)
    lower = (lax.rem(iota(shape, 1), D) <= iota(shape, 0)).astype(F32).astype(BF16)
    return nt(three_parts(decay), lower)


def rows_of(ids_row):
    return jnp.transpose(jnp.broadcast_to(ids_row, (D, D)))


def pack_meta(decay, first, last):
    row = iota((8, D), 0)
    ids = jnp.where(row == 0, first, jnp.where(row == 1, last, 0.0))
    return jnp.concatenate([*split3(decay), ids], axis=0).astype(BF16)


def unpack_meta(meta):
    meta = meta.astype(F32)
    return meta[0:8] + meta[8:16] + meta[16:24], meta[24:25], meta[25:26]


def same(a, b):
    return (a == b).astype(F32)


def summarise(ids, decay, head_rows, out_ref, cut_ref):
    first, last = ids[:, 0:1], ids[:, D - 1 : D]
    total = nt(three_parts(decay), jnp.ones((D, 3 * D), BF16))
    carried = jnp.exp(total - running_sums(decay)) * same(ids, last)
    for group in range(4):
        keys, values = head_rows(group)
        for i in range(GROUP):
            h = group * GROUP + i
            lanes = slice(i * D, (i + 1) * D)
            keyed = (jnp.transpose(keys[:, lanes].astype(F32)) * carried[h : h + 1]).astype(BF16)
            state = jnp.dot(keyed, values[:, lanes], preferred_element_type=F32)
            out_ref[group, i * D : (i + 1) * D, :] = state.astype(BF16)
        cut_ref[0:GROUP, :] = total[group * GROUP : (group + 1) * GROUP, :]
        cut_ref[GROUP:8, :] = jnp.zeros((8 - GROUP, D), F32)
        out_ref[group, ROWS:PART, :] = pack_meta(
            cut_ref[...], jnp.broadcast_to(first, (1, D)), jnp.broadcast_to(last, (1, D))
        )


def summary_kernel(index, k_ref, v_ref, decay_ref, ids_ref, out_ref, cut_ref):
    decay = decay_ref[pl.ds(pl.multiple_of(index[0] * HALF, HALF), HALF), :]

    def head_rows(group):
        lanes = slice(group * ROWS, (group + 1) * ROWS)
        return k_ref[:, lanes], v_ref[:, lanes]

    summarise(ids_ref[...].astype(F32), decay, head_rows, out_ref, cut_ref)


SUMMARY_COST = pl.CostEstimate(flops=2 * HALF * D**3, bytes_accessed=3 * HALF * D * D * 2, transcendentals=0)


def summaries(half, keys, values, decay, ids):
    whole = lambda shape: pl.BlockSpec(shape, lambda i, s: (0,) * len(shape))
    return pl.pallas_call(
        summary_kernel,
        out_shape=jax.ShapeDtypeStruct((4, PART, D), BF16),
        grid_spec=pltpu.PrefetchScalarGridSpec(
            num_scalar_prefetch=1,
            grid=(1,),
            in_specs=[
                pl.BlockSpec((D, HALF * D), lambda i, s: (0, s[0])),
                pl.BlockSpec((D, HALF * D), lambda i, s: (0, s[0])),
                whole((HEADS, D)),
                whole((1, D)),
            ],
            out_specs=whole((4, PART, D)),
            scratch_shapes=[pltpu.VMEM((8, D), F32)],
        ),
        compiler_params=pltpu.CompilerParams(vmem_limit_bytes=VMEM_LIMIT),
        cost_estimate=SUMMARY_COST,
    )(half, keys, values, decay, ids)


def two_parts(x):
    hi = x.astype(BF16)
    return hi, (x - hi.astype(F32)).astype(BF16)


def intra_kernel(wave, q_ref, k_ref, v_ref, decay_ref, ids_ref, out_ref, factor_ref, column_ref, row_ref, allowed_ref):
    step = pl.program_id(0)

    @pl.when(step == 0)
    def _():
        ids = ids_ref[...].astype(F32)
        row_ref[0:HEADS, :] = running_sums(decay_ref[...])
        row_ref[HEADS:D, :] = jnp.zeros((D - HEADS, D), F32)
        sums = jnp.transpose(row_ref[...])
        documents = rows_of(ids)
        scaling = jnp.exp(sums) * same(documents, ids[:, 0:1])
        for quarter in range(4):
            heads = slice(8 * quarter + GROUP * wave, 8 * quarter + GROUP * (wave + 1))
            column_ref[quarter, :, 0:GROUP] = sums[:, heads]
            factor_ref[quarter] = jnp.concatenate(two_parts(scaling[:, heads]), axis=1)
        allowed_ref[...] = ((iota((D, D), 1) <= iota((D, D), 0)) & (documents == ids)).astype(F32)

    allowed = allowed_ref[...] > 0.0
    columns = column_ref[step]
    rows = row_ref[pl.ds(pl.multiple_of(8 * step, 8), 8), :]
    for i in range(GROUP):
        h = GROUP * wave + i
        lanes = slice(i * D, (i + 1) * D)
        spread = jnp.minimum(columns[:, i : i + 1] - rows[h : h + 1, :], 0.0)
        weighting = jnp.where(allowed, jnp.exp(spread), 0.0)
        keys = jnp.transpose(k_ref[:, lanes].astype(F32)).astype(BF16)
        attn = (jnp.dot(q_ref[:, lanes], keys, preferred_element_type=F32) * weighting).astype(BF16)
        out_ref[0, :, lanes] = jnp.dot(attn, v_ref[:, lanes], preferred_element_type=F32)


def intra_term(wave, queries, keys, values, decay, ids):
    block = pl.BlockSpec((D, ROWS), lambda i: (0, 2 * i + wave))
    return pl.pallas_call(
        functools.partial(intra_kernel, wave),
        out_shape=[jax.ShapeDtypeStruct((4, D, ROWS), F32), jax.ShapeDtypeStruct((4, D, 2 * GROUP), BF16)],
        grid=(4,),
        in_specs=[
            block,
            block,
            block,
            pl.BlockSpec((HEADS, D), lambda i: (0, 0)),
            pl.BlockSpec((1, D), lambda i: (0, 0)),
        ],
        out_specs=[
            pl.BlockSpec((1, D, ROWS), lambda i: (i, 0, 0)),
            pl.BlockSpec((4, D, 2 * GROUP), lambda i: (0, 0, 0)),
        ],
        scratch_shapes=[pltpu.VMEM((4, D, 8), F32), pltpu.VMEM((D, D), F32), pltpu.VMEM((D, D), F32)],
        compiler_params=pltpu.CompilerParams(vmem_limit_bytes=INTRA_LIMIT),
        cost_estimate=pl.CostEstimate(
            flops=2 * HEADS * D**3, bytes_accessed=5 * HALF * D * D * 2, transcendentals=HALF * D * D
        ),
    )(queries, keys, values, decay, ids)


def chip_kernel(index, own_ref, other_ref, *out_refs):
    y, core = index[0], index[1]
    is_one = core == 1
    for step in range(4):
        group = lax.rem(y + step, 4)
        decay_own, first_own, last_own = unpack_meta(own_ref[group, ROWS:PART, :])
        decay_other, first_other, last_other = unpack_meta(other_ref[group, ROWS:PART, :])
        joined = same(last_own, last_other)
        later = jnp.where(is_one, decay_own, decay_other)
        passed = jnp.exp(later) * joined
        weight_own = jnp.where(is_one, 1.0, passed)
        weight_other = jnp.where(is_one, passed, 1.0)
        for i in range(GROUP):
            rows = slice(i * D, (i + 1) * D)
            out_refs[step][rows, :] = (
                weight_own[i : i + 1] * own_ref[group, rows, :].astype(F32)
                + weight_other[i : i + 1] * other_ref[group, rows, :].astype(F32)
            ).astype(BF16)
        out_refs[step][ROWS:PART, :] = pack_meta(
            decay_own + decay_other,
            jnp.where(is_one, first_other, first_own),
            jnp.where(is_one, last_own, last_other),
        )


def small_call(kernel, index, operands, outs, scratch=(), after=()):
    whole = lambda shape: pl.BlockSpec(shape, lambda i, s: (0,) * len(shape))
    size = sum(a.size * a.dtype.itemsize for a in operands)
    many, extra = len(operands), len(after)

    def body(index, *refs):
        kernel(index, *refs[:many], *refs[many + extra :])

    return pl.pallas_call(
        body,
        out_shape=[jax.ShapeDtypeStruct(shape, dtype) for shape, dtype in outs],
        grid_spec=pltpu.PrefetchScalarGridSpec(
            num_scalar_prefetch=1,
            grid=(1,),
            in_specs=[whole(a.shape) for a in operands] + [pl.BlockSpec(memory_space=pl.ANY)] * extra,
            out_specs=[whole(shape) for shape, _ in outs],
            scratch_shapes=list(scratch),
        ),
        compiler_params=pltpu.CompilerParams(vmem_limit_bytes=VMEM_LIMIT),
        cost_estimate=pl.CostEstimate(flops=size, bytes_accessed=2 * size, transcendentals=0),
    )(index, *operands, *after)


def in_order(y, slots, ordered_ref):
    for step in range(4):
        ordered_ref[lax.rem(y + 4 - step, 4)] = slots[step][...]


def row_kernel(index, *refs):
    *slots, out_ref, ordered_ref = refs
    in_order(index[0], slots, ordered_ref)
    metas = [unpack_meta(ordered_ref[c, ROWS:PART, :]) for c in range(4)]
    weights, after = [None] * 4, jnp.zeros((8, D), F32)
    for c in (3, 2, 1, 0):
        weights[c] = jnp.exp(after) * same(metas[c][2], metas[3][2])
        after = after + metas[c][0]
    row = iota((16, D), 0)
    for i in range(GROUP):
        rows = slice(i * D, (i + 1) * D)
        state = sum(weights[c][i : i + 1] * ordered_ref[c, rows, :].astype(F32) for c in range(4)).astype(BF16)
        out_ref[2 * i, 0 : D // 2, :] = state[0 : D // 2]
        out_ref[2 * i + 1, 0 : D // 2, :] = state[D // 2 :]
        hi, mid, low = split3(after[i : i + 1])
        meta = jnp.zeros((16, D), F32)
        for at, value in enumerate((hi, mid, low, metas[0][1], metas[3][2])):
            meta = jnp.where(row == at, value, meta)
        out_ref[2 * i, D // 2 :, :] = meta.astype(BF16)
        out_ref[2 * i + 1, D // 2 :, :] = meta.astype(BF16)


def scan_kernel(index, in_ref, out_ref):
    del index
    state = jnp.zeros((D // 2, D), F32)
    before = jnp.full((1, D), -1.0, F32)
    for z in range(NZ):
        meta = in_ref[z, D // 2 :, :].astype(F32)
        decay, first, last = meta[0:1] + meta[1:2] + meta[2:3], meta[3:4], meta[4:5]
        state = state * same(before, first)
        out_ref[z] = state.astype(BF16)
        state = jnp.exp(decay) * same(first, last) * state + in_ref[z, 0 : D // 2, :].astype(F32)
        before = last


def spread_kernel(index, state_ref, *refs):
    *slots, out0, out1, out2, out3, ordered_ref, result_ref = refs
    y = index[0]
    in_order(y, slots, ordered_ref)
    metas = [unpack_meta(ordered_ref[c, ROWS:PART, :]) for c in range(4)]
    passing = [jnp.exp(decay) * same(first, last) for decay, first, last in metas]
    joined = [None] + [same(metas[c - 1][2], metas[c][1]) for c in (1, 2, 3)]
    for i in range(GROUP):
        rows = slice(i * D, (i + 1) * D)
        state = state_ref[rows, :].astype(F32)
        result_ref[0, rows, :] = state.astype(BF16)
        for c in (1, 2, 3):
            state = passing[c - 1][i : i + 1] * state + ordered_ref[c - 1, rows, :].astype(F32)
            state = state * joined[c]
            result_ref[c, rows, :] = state.astype(BF16)
    for step, out_ref in enumerate((out0, out1, out2, out3)):
        out_ref[...] = result_ref[lax.rem(y + step, 4)]


def core_kernel(index, own_ref, other_ref, s0, s1, s2, s3, out_ref):
    y, core, target = index[0], index[1], index[2]
    is_one = core == 1

    @pl.when(target == 0)
    def _():
        for step, slot in enumerate((s0, s1, s2, s3)):
            out_ref[lax.rem(y + 4 - step, 4)] = slot[...]

    @pl.when(target == 1)
    def _():
        for step, slot in enumerate((s0, s1, s2, s3)):
            group = lax.rem(y + 4 - step, 4)
            decay_own, first_own, last_own = unpack_meta(own_ref[group, ROWS:PART, :])
            decay_other, first_other, last_other = unpack_meta(other_ref[group, ROWS:PART, :])
            decay = jnp.where(is_one, decay_other, decay_own)
            first0 = jnp.where(is_one, first_other, first_own)
            last0 = jnp.where(is_one, last_other, last_own)
            first1 = jnp.where(is_one, first_own, first_other)
            joined = same(last0, first1)
            passing = jnp.exp(decay) * same(first0, last0) * joined
            for i in range(GROUP):
                rows = slice(i * D, (i + 1) * D)
                earlier = jnp.where(is_one, other_ref[group, rows, :], own_ref[group, rows, :]).astype(F32)
                later = passing[i : i + 1] * slot[rows, :].astype(F32) + joined * earlier
                out_ref[group, rows, :] = later.astype(BF16)


def attend_kernel(
    wave, index, q_ref, intra_ref, mine_ref, other_ref, factor_ref, gain_ref, *refs
):
    *out_refs, queries, intra, sem = refs
    copies = []
    for step in range(4):
        quarter = lax.rem(index[0] + step, 4)
        lanes = pl.ds(pl.multiple_of((2 * quarter + wave) * ROWS, ROWS), ROWS)
        copies.append(
            [
                pltpu.make_async_copy(q_ref.at[:, lanes], queries.at[step], sem.at[0, step]),
                pltpu.make_async_copy(intra_ref.at[quarter], intra.at[step], sem.at[1, step]),
            ]
        )
    for pair in copies:
        for copy in pair:
            copy.start()
    shape = (2 * GROUP, ROWS)
    spreading = (lax.rem(iota(shape, 0), GROUP) == iota(shape, 1) // D).astype(F32).astype(BF16)
    for step in range(4):
        quarter = lax.rem(index[0] + step, 4)
        group = 2 * quarter + wave
        use_mine = (quarter // 2) == index[1]
        factors = jnp.dot(factor_ref[quarter], spreading, preferred_element_type=F32)
        gain = gain_ref[group]
        for copy in copies[step]:
            copy.wait()
        for i in range(GROUP):
            lanes = slice(i * D, (i + 1) * D)
            at = lax.rem(group, 4)
            state = jnp.where(use_mine, mine_ref[at, lanes, :], other_ref[at, lanes, :])
            inter = jnp.dot(queries[step, :, lanes], state, preferred_element_type=F32)
            total = intra[step, :, lanes] + inter * factors[:, lanes]
            power = jnp.mean(total * total, axis=1, keepdims=True)
            out_refs[step][:, lanes] = (
                total * lax.rsqrt(power + EPSILON) * gain[:, lanes].astype(F32)
            ).astype(BF16)


def attend(wave, index, queries, intra, factors, mine, other, gain):
    whole = lambda shape: pl.BlockSpec(shape, lambda i, s: (0,) * len(shape))
    anywhere = pl.BlockSpec(memory_space=pl.ANY)
    return pl.pallas_call(
        functools.partial(attend_kernel, wave),
        out_shape=[jax.ShapeDtypeStruct((D, ROWS), BF16)] * 4,
        grid_spec=pltpu.PrefetchScalarGridSpec(
            num_scalar_prefetch=1,
            grid=(1,),
            in_specs=[
                anywhere,
                anywhere,
                whole(mine.shape),
                whole(other.shape),
                whole(factors.shape),
                whole(gain.shape),
            ],
            out_specs=[whole((D, ROWS))] * 4,
            scratch_shapes=[
                pltpu.VMEM((4, D, ROWS), BF16),
                pltpu.VMEM((4, D, ROWS), F32),
                pltpu.SemaphoreType.DMA((2, 4)),
            ],
        ),
        compiler_params=pltpu.CompilerParams(vmem_limit_bytes=ATTEND_LIMIT),
        cost_estimate=pl.CostEstimate(
            flops=HEADS * D**3, bytes_accessed=4 * HEADS * D * D * 2, transcendentals=HEADS * D
        ),
    )(index, queries, intra, mine, other, factors, gain)


def layers_kernel(wave, index, tokens_ref, *refs):
    *slots, out0, out1, out2, out3, ordered_ref = refs
    phase = index[0]
    in_order(phase, slots, ordered_ref)
    current = tokens_ref[:, wave * ROWS : (wave + 1) * ROWS].astype(F32)
    for s in range(4):
        rounded = (current + ordered_ref[s].astype(F32)).astype(BF16)
        ordered_ref[s] = rounded
        current = rounded.astype(F32)
    for step, out_ref in enumerate((out0, out1, out2, out3)):
        out_ref[...] = ordered_ref[lax.rem(phase + step, 4)]


def place_kernel(index, *refs):
    *slots, out_ref, sem = refs
    copies = []
    for n, slot in enumerate(slots):
        wave, step = n // 4, n % 4
        quarter = lax.rem(index[0] + 4 - step, 4)
        lanes = pl.ds(pl.multiple_of((2 * quarter + wave) * ROWS, ROWS), ROWS)
        copies.append(pltpu.make_async_copy(slot, out_ref.at[:, lanes], sem.at[n]))
    for copy in copies:
        copy.start()
    for copy in copies:
        copy.wait()


def place(index, slots):
    return pl.pallas_call(
        place_kernel,
        out_shape=jax.ShapeDtypeStruct((D, HEADS * D), BF16),
        grid_spec=pltpu.PrefetchScalarGridSpec(
            num_scalar_prefetch=1,
            grid=(1,),
            in_specs=[pl.BlockSpec(memory_space=pl.ANY)] * 8,
            out_specs=pl.BlockSpec(memory_space=pl.ANY),
            scratch_shapes=[pltpu.SemaphoreType.DMA((8,))],
        ),
        compiler_params=pltpu.CompilerParams(vmem_limit_bytes=VMEM_LIMIT),
        cost_estimate=pl.CostEstimate(flops=0, bytes_accessed=4 * HEADS * D * D, transcendentals=0),
    )(index, *slots)


def ring_exchange(slots, axis):
    size = lax.axis_size(axis)
    moved = [
        lax.ppermute(slots[d], axis, [(i, (i + d) % size) for i in range(size)]) for d in range(1, len(slots))
    ]
    return [slots[0], *moved]


def swap_cores(array):
    return lax.ppermute(array, "core", [(0, 1), (1, 0)])


def local(tokens, queries, keys_in, values, norm_gain, log_decay, doc_ids):
    phase, z, y, core = (lax.axis_index(name) for name in ("phase", "z", "y", "core"))
    queries, keys, values, decay = queries[0, 0], keys_in[0, 0], values[0, 0], log_decay[0, 0]
    here = jnp.stack([y, core, z]).astype(jnp.int32)

    sending = summaries(jnp.stack([1 - core]), keys, values, decay, doc_ids)
    other = swap_cores(sending)
    own = summaries(jnp.stack([core]), keys, values, decay, doc_ids)

    part = ((PART, D), BF16)
    slots = ring_exchange(small_call(chip_kernel, here, [own, other], [part] * 4), "y")
    intra = [intra_term(wave, queries, keys, values, decay, doc_ids) for wave in range(2)]

    (parts,) = small_call(
        row_kernel, here, slots, [((NZ, D // 2 + 16, D), BF16)], [pltpu.VMEM((4, PART, D), BF16)], intra[0][1:]
    )
    parts = lax.all_to_all(parts, "z", split_axis=0, concat_axis=0, tiled=True)
    (states,) = small_call(scan_kernel, here, [parts], [((NZ, D // 2, D), BF16)])
    states = lax.all_to_all(states, "z", split_axis=0, concat_axis=0, tiled=True)
    spread = small_call(
        spread_kernel,
        here,
        [states.reshape(ROWS, D), *slots],
        [((ROWS, D), BF16)] * 4,
        [pltpu.VMEM((4, PART, D), BF16), pltpu.VMEM((4, ROWS, D), BF16)],
    )
    spread = ring_exchange(spread, "y")
    out = [((4, ROWS, D), BF16)]
    to_other = jnp.stack([y, core, 1 - core]).astype(jnp.int32)
    (send,) = small_call(core_kernel, to_other, [own, other, *spread], out, after=intra[1][1:])
    theirs = swap_cores(send)
    (mine,) = small_call(core_kernel, jnp.stack([y, core, core]).astype(jnp.int32), [own, other, *spread], out)

    at = jnp.stack([phase, core]).astype(jnp.int32)
    gain = norm_gain.reshape(8, 1, ROWS)
    pieces = []
    for wave in range(2):
        normed = ring_exchange(attend(wave, at, queries, *intra[wave], mine, theirs, gain), "phase")
        sums = small_call(
            functools.partial(layers_kernel, wave),
            at,
            [tokens[0], *normed],
            [((D, ROWS), BF16)] * 4,
            [pltpu.VMEM((4, D, ROWS), BF16)],
        )
        pieces += ring_exchange(sums, "phase")
    return place(at, pieces)[None, None]


def solution(mesh):
    grid = Mesh(mesh.devices.reshape(4, NZ, 4, 2), ("phase", "z", "y", "core"))
    ctx = ("z", "y", "core")
    rows = P("phase", None, ctx, None)
    return jax.shard_map(
        local,
        mesh=grid,
        in_specs=(
            P(None, ctx, "phase"),
            rows,
            rows,
            rows,
            P("phase", None),
            P("phase", None, None, ctx),
            P(None, ctx),
        ),
        out_specs=rows,
        check_vma=False,
    )
```

```python
import functools

import jax
import jax.numpy as jnp
from jax import lax
from jax.experimental import pallas as pl
from jax.experimental.pallas import tpu as pltpu
from jax.sharding import Mesh
from jax.sharding import PartitionSpec as P

EPSILON = 1e-05
F32, BF16 = jnp.float32, jnp.bfloat16
D = 128
HEADS = 32
HALF = HEADS // 2
GROUP = HALF // 4
NZ = 8
META = 32
ROWS = GROUP * D
PART = ROWS + META
PHASE, Y, CORE = 0, 1, 2
VMEM_LIMIT = 16 * 1024 * 1024


def nt(a, b):
    return lax.dot_general(a, b, (((1,), (1,)), ((), ())), preferred_element_type=F32)


def iota(shape, axis):
    return lax.broadcasted_iota(jnp.int32, shape, axis)


def split3(x):
    hi = x.astype(BF16).astype(F32)
    mid = (x - hi).astype(BF16).astype(F32)
    return hi, mid, x - hi - mid


def three_parts(x):
    return jnp.concatenate([part.astype(BF16) for part in split3(x)], axis=1)


def running_sums(decay):
    shape = (D, 3 * D)
    lower = (lax.rem(iota(shape, 1), D) <= iota(shape, 0)).astype(F32).astype(BF16)
    return nt(three_parts(decay), lower)


def rows_of(ids_row):
    return jnp.transpose(jnp.broadcast_to(ids_row, (D, D)))


def pack_meta(decay, first, last):
    row = iota((8, D), 0)
    ids = jnp.where(row == 0, first, jnp.where(row == 1, last, 0.0))
    return jnp.concatenate([*split3(decay), ids], axis=0).astype(BF16)


def unpack_meta(meta):
    meta = meta.astype(F32)
    return meta[0:8] + meta[8:16] + meta[16:24], meta[24:25], meta[25:26]


def same(a, b):
    return (a == b).astype(F32)


def summary_kernel(of_other, index, k_ref, v_ref, decay_ref, ids_ref, out_ref, cut_ref):
    half = 1 - index[CORE] if of_other else index[CORE]
    ids = ids_ref[...].astype(F32)
    first, last = ids[:, 0:1], ids[:, D - 1 : D]
    decay = decay_ref[pl.ds(pl.multiple_of(half * HALF, HALF), HALF), :]
    total = nt(three_parts(decay), jnp.ones((D, 3 * D), BF16))
    carried = jnp.exp(total - running_sums(decay)) * same(ids, last)
    for group in range(4):
        for i in range(GROUP):
            h = group * GROUP + i
            lanes = slice(h * D, (h + 1) * D)
            keyed = (jnp.transpose(k_ref[:, lanes].astype(F32)) * carried[h : h + 1]).astype(BF16)
            state = jnp.dot(keyed, v_ref[:, lanes], preferred_element_type=F32)
            out_ref[group, i * D : (i + 1) * D, :] = state.astype(BF16)
        cut_ref[0:GROUP, :] = total[group * GROUP : (group + 1) * GROUP, :]
        cut_ref[GROUP:8, :] = jnp.zeros((8 - GROUP, D), F32)
        out_ref[group, ROWS:PART, :] = pack_meta(
            cut_ref[...], jnp.broadcast_to(first, (1, D)), jnp.broadcast_to(last, (1, D))
        )


def summaries(of_other, index, keys, values, decay, ids):
    whole = lambda shape: pl.BlockSpec(shape, lambda i, s: (0,) * len(shape))
    block = pl.BlockSpec((D, HALF * D), lambda i, s: (0, 1 - s[CORE] if of_other else s[CORE]))
    return pl.pallas_call(
        functools.partial(summary_kernel, of_other),
        out_shape=jax.ShapeDtypeStruct((4, PART, D), BF16),
        grid_spec=pltpu.PrefetchScalarGridSpec(
            num_scalar_prefetch=1,
            grid=(1,),
            in_specs=[block, block, whole((HEADS, D)), whole((1, D))],
            out_specs=whole((4, PART, D)),
            scratch_shapes=[pltpu.VMEM((8, D), F32)],
        ),
        compiler_params=pltpu.CompilerParams(vmem_limit_bytes=VMEM_LIMIT),
        cost_estimate=pl.CostEstimate(flops=HEADS * D**3, bytes_accessed=3 * HALF * D * D * 2, transcendentals=0),
    )(index, keys, values, decay, ids)


def two_parts(x):
    hi = x.astype(BF16)
    return hi, (x - hi.astype(F32)).astype(BF16)


def intra_kernel(
    wave, q_ref, k_ref, v_ref, decay_ref, ids_ref, out_ref, factor_ref, column_ref, row_ref, allowed_ref
):
    step = pl.program_id(0)

    @pl.when(step == 0)
    def _():
        ids = ids_ref[...].astype(F32)
        row_ref[0:HEADS, :] = running_sums(decay_ref[...])
        row_ref[HEADS:D, :] = jnp.zeros((D - HEADS, D), F32)
        sums = jnp.transpose(row_ref[...])
        documents = rows_of(ids)
        scaling = jnp.exp(sums) * same(documents, ids[:, 0:1])
        for quarter in range(4):
            heads = slice(8 * quarter + GROUP * wave, 8 * quarter + GROUP * (wave + 1))
            column_ref[quarter, :, 0:GROUP] = sums[:, heads]
            factor_ref[quarter] = jnp.concatenate(two_parts(scaling[:, heads]), axis=1)
        allowed_ref[...] = ((iota((D, D), 1) <= iota((D, D), 0)) & (documents == ids)).astype(F32)

    allowed = allowed_ref[...] > 0.0
    columns = column_ref[step]
    rows = row_ref[pl.ds(pl.multiple_of(8 * step, 8), 8), :]
    for i in range(GROUP):
        h = GROUP * wave + i
        lanes = slice(i * D, (i + 1) * D)
        spread = jnp.minimum(columns[:, i : i + 1] - rows[h : h + 1, :], 0.0)
        weighting = jnp.where(allowed, jnp.exp(spread), 0.0)
        keys = jnp.transpose(k_ref[:, lanes].astype(F32)).astype(BF16)
        attn = (jnp.dot(q_ref[:, lanes], keys, preferred_element_type=F32) * weighting).astype(BF16)
        out_ref[0, :, lanes] = jnp.dot(attn, v_ref[:, lanes], preferred_element_type=F32)


def intra_term(wave, queries, keys, values, decay, ids):
    block = pl.BlockSpec((D, ROWS), lambda i: (0, 2 * i + wave))
    return pl.pallas_call(
        functools.partial(intra_kernel, wave),
        out_shape=[jax.ShapeDtypeStruct((4, D, ROWS), F32), jax.ShapeDtypeStruct((4, D, 2 * GROUP), BF16)],
        grid=(4,),
        in_specs=[
            block,
            block,
            block,
            pl.BlockSpec((HEADS, D), lambda i: (0, 0)),
            pl.BlockSpec((1, D), lambda i: (0, 0)),
        ],
        out_specs=[
            pl.BlockSpec((1, D, ROWS), lambda i: (i, 0, 0)),
            pl.BlockSpec((4, D, 2 * GROUP), lambda i: (0, 0, 0)),
        ],
        scratch_shapes=[pltpu.VMEM((4, D, 8), F32), pltpu.VMEM((D, D), F32), pltpu.VMEM((D, D), F32)],
        compiler_params=pltpu.CompilerParams(vmem_limit_bytes=VMEM_LIMIT),
        cost_estimate=pl.CostEstimate(
            flops=2 * HEADS * D**3, bytes_accessed=5 * HALF * D * D * 2, transcendentals=HALF * D * D
        ),
    )(queries, keys, values, decay, ids)


def chip_kernel(index, own_ref, other_ref, *out_refs):
    y, core = index[Y], index[CORE]
    is_one = core == 1
    for step in range(4):
        group = lax.rem(y + step, 4)
        decay_own, first_own, last_own = unpack_meta(own_ref[group, ROWS:PART, :])
        decay_other, first_other, last_other = unpack_meta(other_ref[group, ROWS:PART, :])
        joined = same(last_own, last_other)
        later = jnp.where(is_one, decay_own, decay_other)
        passed = jnp.exp(later) * joined
        weight_own = jnp.where(is_one, 1.0, passed)
        weight_other = jnp.where(is_one, passed, 1.0)
        for i in range(GROUP):
            rows = slice(i * D, (i + 1) * D)
            out_refs[step][rows, :] = (
                weight_own[i : i + 1] * own_ref[group, rows, :].astype(F32)
                + weight_other[i : i + 1] * other_ref[group, rows, :].astype(F32)
            ).astype(BF16)
        out_refs[step][ROWS:PART, :] = pack_meta(
            decay_own + decay_other,
            jnp.where(is_one, first_other, first_own),
            jnp.where(is_one, last_own, last_other),
        )


def small_call(kernel, index, operands, outs, scratch=(), after=()):
    whole = lambda shape: pl.BlockSpec(shape, lambda i, s: (0,) * len(shape))
    size = sum(a.size * a.dtype.itemsize for a in operands)
    many, extra = len(operands), len(after)

    def body(index, *refs):
        kernel(index, *refs[:many], *refs[many + extra :])

    return pl.pallas_call(
        body,
        out_shape=[jax.ShapeDtypeStruct(shape, dtype) for shape, dtype in outs],
        grid_spec=pltpu.PrefetchScalarGridSpec(
            num_scalar_prefetch=1,
            grid=(1,),
            in_specs=[whole(a.shape) for a in operands] + [pl.BlockSpec(memory_space=pl.ANY)] * extra,
            out_specs=[whole(shape) for shape, _ in outs],
            scratch_shapes=list(scratch),
        ),
        compiler_params=pltpu.CompilerParams(vmem_limit_bytes=VMEM_LIMIT),
        cost_estimate=pl.CostEstimate(flops=size, bytes_accessed=2 * size, transcendentals=0),
    )(index, *operands, *after)


def in_order(y, slots, ordered_ref):
    for step in range(4):
        ordered_ref[lax.rem(y + 4 - step, 4)] = slots[step][...]


def row_kernel(index, *refs):
    *slots, out_ref, ordered_ref = refs
    in_order(index[Y], slots, ordered_ref)
    metas = [unpack_meta(ordered_ref[c, ROWS:PART, :]) for c in range(4)]
    weights, after = [None] * 4, jnp.zeros((8, D), F32)
    for c in (3, 2, 1, 0):
        weights[c] = jnp.exp(after) * same(metas[c][2], metas[3][2])
        after = after + metas[c][0]
    row = iota((16, D), 0)
    for i in range(GROUP):
        rows = slice(i * D, (i + 1) * D)
        state = sum(weights[c][i : i + 1] * ordered_ref[c, rows, :].astype(F32) for c in range(4)).astype(BF16)
        out_ref[2 * i, 0 : D // 2, :] = state[0 : D // 2]
        out_ref[2 * i + 1, 0 : D // 2, :] = state[D // 2 :]
        hi, mid, low = split3(after[i : i + 1])
        meta = jnp.zeros((16, D), F32)
        for at, value in enumerate((hi, mid, low, metas[0][1], metas[3][2])):
            meta = jnp.where(row == at, value, meta)
        out_ref[2 * i, D // 2 :, :] = meta.astype(BF16)
        out_ref[2 * i + 1, D // 2 :, :] = meta.astype(BF16)


def scan_kernel(index, in_ref, out_ref):
    del index
    state = jnp.zeros((D // 2, D), F32)
    before = jnp.full((1, D), -1.0, F32)
    for z in range(NZ):
        meta = in_ref[z, D // 2 :, :].astype(F32)
        decay, first, last = meta[0:1] + meta[1:2] + meta[2:3], meta[3:4], meta[4:5]
        state = state * same(before, first)
        out_ref[z] = state.astype(BF16)
        state = jnp.exp(decay) * same(first, last) * state + in_ref[z, 0 : D // 2, :].astype(F32)
        before = last


def spread_kernel(index, state_ref, *refs):
    *slots, out0, out1, out2, out3, ordered_ref, result_ref = refs
    y = index[Y]
    in_order(y, slots, ordered_ref)
    metas = [unpack_meta(ordered_ref[c, ROWS:PART, :]) for c in range(4)]
    passing = [jnp.exp(decay) * same(first, last) for decay, first, last in metas]
    joined = [None] + [same(metas[c - 1][2], metas[c][1]) for c in (1, 2, 3)]
    for i in range(GROUP):
        rows = slice(i * D, (i + 1) * D)
        state = state_ref[rows, :].astype(F32)
        result_ref[0, rows, :] = state.astype(BF16)
        for c in (1, 2, 3):
            state = passing[c - 1][i : i + 1] * state + ordered_ref[c - 1, rows, :].astype(F32)
            state = state * joined[c]
            result_ref[c, rows, :] = state.astype(BF16)
    for step, out_ref in enumerate((out0, out1, out2, out3)):
        out_ref[...] = result_ref[lax.rem(y + step, 4)]


def core_kernel(of_other, index, own_ref, other_ref, s0, s1, s2, s3, out_ref):
    y, core = index[Y], index[CORE]
    is_one = core == 1
    target = 1 - core if of_other else core

    @pl.when(target == 0)
    def _():
        for step, slot in enumerate((s0, s1, s2, s3)):
            out_ref[lax.rem(y + 4 - step, 4)] = slot[...]

    @pl.when(target == 1)
    def _():
        for step, slot in enumerate((s0, s1, s2, s3)):
            group = lax.rem(y + 4 - step, 4)
            decay_own, first_own, last_own = unpack_meta(own_ref[group, ROWS:PART, :])
            decay_other, first_other, last_other = unpack_meta(other_ref[group, ROWS:PART, :])
            decay = jnp.where(is_one, decay_other, decay_own)
            first0 = jnp.where(is_one, first_other, first_own)
            last0 = jnp.where(is_one, last_other, last_own)
            first1 = jnp.where(is_one, first_own, first_other)
            joined = same(last0, first1)
            passing = jnp.exp(decay) * same(first0, last0) * joined
            for i in range(GROUP):
                rows = slice(i * D, (i + 1) * D)
                earlier = jnp.where(is_one, other_ref[group, rows, :], own_ref[group, rows, :]).astype(F32)
                later = passing[i : i + 1] * slot[rows, :].astype(F32) + joined * earlier
                out_ref[group, rows, :] = later.astype(BF16)


def attend_kernel(wave, index, q_ref, intra_ref, factor_ref, mine_ref, other_ref, gain_ref, *out_refs):
    shape = (2 * GROUP, ROWS)
    spreading = (lax.rem(iota(shape, 0), GROUP) == iota(shape, 1) // D).astype(F32).astype(BF16)
    for step in range(4):
        quarter = lax.rem(index[PHASE] + step, 4)
        group = 2 * quarter + wave
        at = lax.rem(group, 4)
        use_mine = (quarter // 2) == index[CORE]
        factors = jnp.dot(factor_ref[quarter], spreading, preferred_element_type=F32)
        gain = gain_ref[group]
        for i in range(GROUP):
            lanes = slice(i * D, (i + 1) * D)
            state = jnp.where(use_mine, mine_ref[at, lanes, :], other_ref[at, lanes, :])
            queries = q_ref[:, pl.ds(pl.multiple_of(group * ROWS + i * D, D), D)]
            inter = jnp.dot(queries, state, preferred_element_type=F32)
            total = intra_ref[quarter, :, lanes] + inter * factors[:, lanes]
            power = jnp.mean(total * total, axis=1, keepdims=True)
            out_refs[step][:, lanes] = (
                total * lax.rsqrt(power + EPSILON) * gain[:, lanes].astype(F32)
            ).astype(BF16)


def attend(wave, index, *operands):
    return small_call(functools.partial(attend_kernel, wave), index, operands, [((D, ROWS), BF16)] * 4)


def layers_kernel(wave, index, tokens_ref, *refs):
    *slots, out0, out1, out2, out3, ordered_ref = refs
    phase = index[PHASE]
    in_order(phase, slots, ordered_ref)
    current = tokens_ref[:, wave * ROWS : (wave + 1) * ROWS].astype(F32)
    for s in range(4):
        rounded = (current + ordered_ref[s].astype(F32)).astype(BF16)
        ordered_ref[s] = rounded
        current = rounded.astype(F32)
    for step, out_ref in enumerate((out0, out1, out2, out3)):
        out_ref[...] = ordered_ref[lax.rem(phase + step, 4)]


def place_kernel(wave, index, *refs):
    slots, out_ref, sem = refs[:4], refs[-2], refs[-1]
    copies = []
    for step, slot in enumerate(slots):
        quarter = lax.rem(index[PHASE] + 4 - step, 4)
        lanes = pl.ds(pl.multiple_of((2 * quarter + wave) * ROWS, ROWS), ROWS)
        copies.append(pltpu.make_async_copy(slot, out_ref.at[:, lanes], sem.at[step]))
    for copy in copies:
        copy.start()
    for copy in copies:
        copy.wait()


def place(wave, index, slots, out=None):
    given = [] if out is None else [out]
    return pl.pallas_call(
        functools.partial(place_kernel, wave),
        out_shape=jax.ShapeDtypeStruct((D, HEADS * D), BF16),
        grid_spec=pltpu.PrefetchScalarGridSpec(
            num_scalar_prefetch=1,
            grid=(1,),
            in_specs=[pl.BlockSpec(memory_space=pl.ANY)] * (4 + len(given)),
            out_specs=pl.BlockSpec(memory_space=pl.ANY),
            scratch_shapes=[pltpu.SemaphoreType.DMA((4,))],
        ),
        input_output_aliases={5: 0} if given else {},
        compiler_params=pltpu.CompilerParams(vmem_limit_bytes=VMEM_LIMIT),
        cost_estimate=pl.CostEstimate(flops=0, bytes_accessed=2 * HEADS * D * D, transcendentals=0),
    )(index, *slots, *given)


def ring_exchange(slots, axis):
    size = lax.axis_size(axis)
    moved = [
        lax.ppermute(slots[d], axis, [(i, (i + d) % size) for i in range(size)]) for d in range(1, len(slots))
    ]
    return [slots[0], *moved]


def swap_cores(array):
    return lax.ppermute(array, "core", [(0, 1), (1, 0)])


def local(tokens, queries, keys_in, values, norm_gain, log_decay, doc_ids):
    index = jnp.stack([lax.axis_index(name) for name in ("phase", "y", "core")]).astype(jnp.int32)
    queries, keys, values, decay = queries[0, 0], keys_in[0, 0], values[0, 0], log_decay[0, 0]
    gain = norm_gain.reshape(8, 1, ROWS)

    other = swap_cores(summaries(True, index, keys, values, decay, doc_ids))
    own = summaries(False, index, keys, values, decay, doc_ids)

    part, group_states = ((PART, D), BF16), ((ROWS, D), BF16)
    slots = ring_exchange(small_call(chip_kernel, index, [own, other], [part] * 4), "y")
    intra = [intra_term(wave, queries, keys, values, decay, doc_ids) for wave in range(2)]

    (parts,) = small_call(
        row_kernel, index, slots, [((NZ, D // 2 + 16, D), BF16)], [pltpu.VMEM((4, PART, D), BF16)], intra[0][:1]
    )
    parts = lax.all_to_all(parts, "z", split_axis=0, concat_axis=0, tiled=True)
    (states,) = small_call(scan_kernel, index, [parts], [((NZ, D // 2, D), BF16)])
    states = lax.all_to_all(states, "z", split_axis=0, concat_axis=0, tiled=True)
    spread = small_call(
        spread_kernel,
        index,
        [states.reshape(ROWS, D), *slots],
        [group_states] * 4,
        [pltpu.VMEM((4, PART, D), BF16), pltpu.VMEM((4, ROWS, D), BF16)],
    )
    spread = ring_exchange(spread, "y")
    for_core = lambda of_other, after: small_call(
        functools.partial(core_kernel, of_other), index, [own, other, *spread], [((4, ROWS, D), BF16)], after=after
    )[0]
    theirs = swap_cores(for_core(True, intra[1][:1]))
    mine = for_core(False, ())

    result = None
    for wave in range(2):
        normed = ring_exchange(attend(wave, index, queries, *intra[wave], mine, theirs, gain), "phase")
        sums = small_call(
            functools.partial(layers_kernel, wave),
            index,
            [tokens[0], *normed],
            [((D, ROWS), BF16)] * 4,
            [pltpu.VMEM((4, D, ROWS), BF16)],
        )
        result = place(wave, index, ring_exchange(sums, "phase"), result)
    return result[None, None]


def solution(mesh):
    grid = Mesh(mesh.devices.reshape(4, NZ, 4, 2), ("phase", "z", "y", "core"))
    ctx = ("z", "y", "core")
    rows = P("phase", None, ctx, None)
    return jax.shard_map(
        local,
        mesh=grid,
        in_specs=(
            P(None, ctx, "phase"),
            rows,
            rows,
            rows,
            P("phase", None),
            P("phase", None, None, ctx),
            P(None, ctx),
        ),
        out_specs=rows,
        check_vma=False,
    )
```

```python
import functools

import jax
import jax.numpy as jnp
from jax import lax
from jax.experimental import pallas as pl
from jax.experimental.pallas import tpu as pltpu
from jax.sharding import Mesh
from jax.sharding import PartitionSpec as P

EPSILON = 1e-05
F32, BF16 = jnp.float32, jnp.bfloat16
D = 128
HEADS = 32
HALF = HEADS // 2
GROUP = HALF // 4
NZ = 8
META = 32
ROWS = GROUP * D
PART = ROWS + META
PAIR = 2 * D + META
PHASE, Y, CORE, Z = 0, 1, 2, 3
VMEM_LIMIT = 16 * 1024 * 1024


def nt(a, b):
    return lax.dot_general(a, b, (((1,), (1,)), ((), ())), preferred_element_type=F32)


def iota(shape, axis):
    return lax.broadcasted_iota(jnp.int32, shape, axis)


def split3(x):
    hi = x.astype(BF16).astype(F32)
    mid = (x - hi).astype(BF16).astype(F32)
    return hi, mid, x - hi - mid


def three_parts(x):
    return jnp.concatenate([part.astype(BF16) for part in split3(x)], axis=1)


def running_sums(decay):
    shape = (D, 3 * D)
    lower = (lax.rem(iota(shape, 1), D) <= iota(shape, 0)).astype(F32).astype(BF16)
    return nt(three_parts(decay), lower)


def rows_of(ids_row):
    return jnp.transpose(jnp.broadcast_to(ids_row, (D, D)))


def pack_meta(decay, first, last):
    row = iota((8, D), 0)
    ids = jnp.where(row == 0, first, jnp.where(row == 1, last, 0.0))
    return jnp.concatenate([*split3(decay), ids], axis=0).astype(BF16)


def unpack_meta(meta):
    meta = meta.astype(F32)
    return meta[0:8] + meta[8:16] + meta[16:24], meta[24:25], meta[25:26]


def same(a, b):
    return (a == b).astype(F32)


def summary_kernel(of_other, index, k_ref, v_ref, decay_ref, ids_ref, out_ref, cut_ref):
    half = 1 - index[CORE] if of_other else index[CORE]
    ids = ids_ref[...].astype(F32)
    first, last = ids[:, 0:1], ids[:, D - 1 : D]
    decay = decay_ref[pl.ds(pl.multiple_of(half * HALF, HALF), HALF), :]
    total = nt(three_parts(decay), jnp.ones((D, 3 * D), BF16))
    carried = jnp.exp(total - running_sums(decay)) * same(ids, last)
    for group in range(4):
        for i in range(GROUP):
            h = group * GROUP + i
            lanes = slice(h * D, (h + 1) * D)
            keyed = (jnp.transpose(k_ref[:, lanes].astype(F32)) * carried[h : h + 1]).astype(BF16)
            state = jnp.dot(keyed, v_ref[:, lanes], preferred_element_type=F32)
            out_ref[group, i * D : (i + 1) * D, :] = state.astype(BF16)
        cut_ref[0:GROUP, :] = total[group * GROUP : (group + 1) * GROUP, :]
        cut_ref[GROUP:8, :] = jnp.zeros((8 - GROUP, D), F32)
        out_ref[group, ROWS:PART, :] = pack_meta(
            cut_ref[...], jnp.broadcast_to(first, (1, D)), jnp.broadcast_to(last, (1, D))
        )


def summaries(of_other, index, keys, values, decay, ids):
    whole = lambda shape: pl.BlockSpec(shape, lambda i, s: (0,) * len(shape))
    block = pl.BlockSpec((D, HALF * D), lambda i, s: (0, 1 - s[CORE] if of_other else s[CORE]))
    return pl.pallas_call(
        functools.partial(summary_kernel, of_other),
        out_shape=jax.ShapeDtypeStruct((4, PART, D), BF16),
        grid_spec=pltpu.PrefetchScalarGridSpec(
            num_scalar_prefetch=1,
            grid=(1,),
            in_specs=[block, block, whole((HEADS, D)), whole((1, D))],
            out_specs=whole((4, PART, D)),
            scratch_shapes=[pltpu.VMEM((8, D), F32)],
        ),
        compiler_params=pltpu.CompilerParams(vmem_limit_bytes=VMEM_LIMIT),
        cost_estimate=pl.CostEstimate(flops=HEADS * D**3, bytes_accessed=3 * HALF * D * D * 2, transcendentals=0),
    )(index, keys, values, decay, ids)


def two_parts(x):
    hi = x.astype(BF16)
    return hi, (x - hi.astype(F32)).astype(BF16)


def intra_kernel(
    wave, q_ref, k_ref, v_ref, decay_ref, ids_ref, out_ref, factor_ref, column_ref, row_ref, allowed_ref
):
    step = pl.program_id(0)

    @pl.when(step == 0)
    def _():
        ids = ids_ref[...].astype(F32)
        row_ref[0:HEADS, :] = running_sums(decay_ref[...])
        row_ref[HEADS:D, :] = jnp.zeros((D - HEADS, D), F32)
        sums = jnp.transpose(row_ref[...])
        documents = rows_of(ids)
        scaling = jnp.exp(sums) * same(documents, ids[:, 0:1])
        for quarter in range(4):
            heads = slice(8 * quarter + GROUP * wave, 8 * quarter + GROUP * (wave + 1))
            column_ref[quarter, :, 0:GROUP] = sums[:, heads]
            factor_ref[quarter] = jnp.concatenate(two_parts(scaling[:, heads]), axis=1)
        allowed_ref[...] = ((iota((D, D), 1) <= iota((D, D), 0)) & (documents == ids)).astype(F32)

    allowed = allowed_ref[...] > 0.0
    columns = column_ref[step]
    rows = row_ref[pl.ds(pl.multiple_of(8 * step, 8), 8), :]
    for i in range(GROUP):
        h = GROUP * wave + i
        lanes = slice(i * D, (i + 1) * D)
        spread = jnp.minimum(columns[:, i : i + 1] - rows[h : h + 1, :], 0.0)
        weighting = jnp.where(allowed, jnp.exp(spread), 0.0)
        keys = jnp.transpose(k_ref[:, lanes].astype(F32)).astype(BF16)
        attn = (jnp.dot(q_ref[:, lanes], keys, preferred_element_type=F32) * weighting).astype(BF16)
        out_ref[0, :, lanes] = jnp.dot(attn, v_ref[:, lanes], preferred_element_type=F32)


def intra_term(wave, queries, keys, values, decay, ids):
    block = pl.BlockSpec((D, ROWS), lambda i: (0, 2 * i + wave))
    return pl.pallas_call(
        functools.partial(intra_kernel, wave),
        out_shape=[jax.ShapeDtypeStruct((4, D, ROWS), F32), jax.ShapeDtypeStruct((4, D, 2 * GROUP), BF16)],
        grid=(4,),
        in_specs=[
            block,
            block,
            block,
            pl.BlockSpec((HEADS, D), lambda i: (0, 0)),
            pl.BlockSpec((1, D), lambda i: (0, 0)),
        ],
        out_specs=[
            pl.BlockSpec((1, D, ROWS), lambda i: (i, 0, 0)),
            pl.BlockSpec((4, D, 2 * GROUP), lambda i: (0, 0, 0)),
        ],
        scratch_shapes=[pltpu.VMEM((4, D, 8), F32), pltpu.VMEM((D, D), F32), pltpu.VMEM((D, D), F32)],
        compiler_params=pltpu.CompilerParams(vmem_limit_bytes=VMEM_LIMIT),
        cost_estimate=pl.CostEstimate(
            flops=2 * HEADS * D**3, bytes_accessed=5 * HALF * D * D * 2, transcendentals=HALF * D * D
        ),
    )(queries, keys, values, decay, ids)


def chip_kernel(index, own_ref, other_ref, *out_refs):
    y, core = index[Y], index[CORE]
    is_one = core == 1
    for step in range(4):
        group = lax.rem(y + step, 4)
        decay_own, first_own, last_own = unpack_meta(own_ref[group, ROWS:PART, :])
        decay_other, first_other, last_other = unpack_meta(other_ref[group, ROWS:PART, :])
        joined = same(last_own, last_other)
        later = jnp.where(is_one, decay_own, decay_other)
        passed = jnp.exp(later) * joined
        weight_own = jnp.where(is_one, 1.0, passed)
        weight_other = jnp.where(is_one, passed, 1.0)
        for i in range(GROUP):
            rows = slice(i * D, (i + 1) * D)
            out_refs[step][rows, :] = (
                weight_own[i : i + 1] * own_ref[group, rows, :].astype(F32)
                + weight_other[i : i + 1] * other_ref[group, rows, :].astype(F32)
            ).astype(BF16)
        out_refs[step][ROWS:PART, :] = pack_meta(
            decay_own + decay_other,
            jnp.where(is_one, first_other, first_own),
            jnp.where(is_one, last_own, last_other),
        )


def small_call(kernel, index, operands, outs, scratch=(), after=()):
    whole = lambda shape: pl.BlockSpec(shape, lambda i, s: (0,) * len(shape))
    size = sum(a.size * a.dtype.itemsize for a in operands)
    many, extra = len(operands), len(after)

    def body(index, *refs):
        kernel(index, *refs[:many], *refs[many + extra :])

    return pl.pallas_call(
        body,
        out_shape=[jax.ShapeDtypeStruct(shape, dtype) for shape, dtype in outs],
        grid_spec=pltpu.PrefetchScalarGridSpec(
            num_scalar_prefetch=1,
            grid=(1,),
            in_specs=[whole(a.shape) for a in operands] + [pl.BlockSpec(memory_space=pl.ANY)] * extra,
            out_specs=[whole(shape) for shape, _ in outs],
            scratch_shapes=list(scratch),
        ),
        compiler_params=pltpu.CompilerParams(vmem_limit_bytes=VMEM_LIMIT),
        cost_estimate=pl.CostEstimate(flops=size, bytes_accessed=2 * size, transcendentals=0),
    )(index, *operands, *after)


def in_order(y, slots, ordered_ref):
    for step in range(4):
        ordered_ref[lax.rem(y + 4 - step, 4)] = slots[step][...]


def row_kernel(index, *refs):
    *slots, send_ref, keep_ref, ordered_ref, state_ref = refs
    in_order(index[Y], slots, ordered_ref)
    metas = [unpack_meta(ordered_ref[c, ROWS:PART, :]) for c in range(4)]
    weights, after = [None] * 4, jnp.zeros((8, D), F32)
    for c in (3, 2, 1, 0):
        weights[c] = jnp.exp(after) * same(metas[c][2], metas[3][2])
        after = after + metas[c][0]
    for i in range(GROUP):
        rows = slice(i * D, (i + 1) * D)
        state = sum(weights[c][i : i + 1] * ordered_ref[c, rows, :].astype(F32) for c in range(4))
        state_ref[i] = state.astype(BF16)
    odd = lax.rem(index[Z], 2)
    turned = jnp.concatenate([after[2:4], after[0:2], after[4:8]], axis=0)
    for out_ref, half in ((send_ref, 1 - odd), (keep_ref, odd)):
        for i in range(2):
            out_ref[i * D : (i + 1) * D, :] = state_ref[2 * half + i]
        out_ref[2 * D : PAIR, :] = pack_meta(jnp.where(half == 0, after, turned), metas[0][1], metas[3][2])


def pair_kernel(index, own_ref, other_ref, out_ref):
    is_odd = lax.rem(index[Z], 2) == 1
    decay_own, first_own, last_own = unpack_meta(own_ref[2 * D : PAIR, :])
    decay_other, first_other, last_other = unpack_meta(other_ref[2 * D : PAIR, :])
    passed = jnp.exp(jnp.where(is_odd, decay_own, decay_other)) * same(last_own, last_other)
    weight_own = jnp.where(is_odd, 1.0, passed)
    weight_other = jnp.where(is_odd, passed, 1.0)
    for i in range(2):
        rows = slice(i * D, (i + 1) * D)
        out_ref[rows, :] = (
            weight_own[i : i + 1] * own_ref[rows, :].astype(F32)
            + weight_other[i : i + 1] * other_ref[rows, :].astype(F32)
        ).astype(BF16)
    out_ref[2 * D : PAIR, :] = pack_meta(
        decay_own + decay_other,
        jnp.where(is_odd, first_other, first_own),
        jnp.where(is_odd, last_own, last_other),
    )


def prefix_kernel(index, own_ref, other_ref, *refs):
    *before, mine_ref, send_ref = refs
    is_odd = lax.rem(index[Z], 2) == 1
    decay_own, first_own, last_own = unpack_meta(own_ref[2 * D : PAIR, :])
    decay_other, first_other, last_other = unpack_meta(other_ref[2 * D : PAIR, :])
    decay0 = jnp.where(is_odd, decay_other, decay_own)
    first0, first1 = jnp.where(is_odd, first_other, first_own), jnp.where(is_odd, first_own, first_other)
    last0 = jnp.where(is_odd, last_other, last_own)
    joined = same(last0, first1)
    passing = jnp.exp(decay0) * same(first0, last0) * joined
    weights, after = [], jnp.zeros((8, D), F32)
    for back, pair in enumerate(before, start=1):
        decay, _, last = unpack_meta(pair[2 * D : PAIR, :])
        weights.append(jnp.where(index[Z] >= 2 * back, jnp.exp(after) * same(last, first0), 0.0))
        after = after + decay
    for i in range(2):
        rows = slice(i * D, (i + 1) * D)
        state = sum(w[i : i + 1] * pair[rows, :].astype(F32) for w, pair in zip(weights, before))
        earlier = jnp.where(is_odd, other_ref[rows, :], own_ref[rows, :]).astype(F32)
        later = passing[i : i + 1] * state + joined * earlier
        mine_ref[rows, :] = jnp.where(is_odd, later, state).astype(BF16)
        send_ref[rows, :] = jnp.where(is_odd, state, later).astype(BF16)


def spread_kernel(index, mine_ref, theirs_ref, *refs):
    *slots, out0, out1, out2, out3, ordered_ref, result_ref = refs
    y, odd = index[Y], lax.rem(index[Z], 2)
    in_order(y, slots, ordered_ref)
    metas = [unpack_meta(ordered_ref[c, ROWS:PART, :]) for c in range(4)]
    passing = [jnp.exp(decay) * same(first, last) for decay, first, last in metas]
    joined = [None] + [same(metas[c - 1][2], metas[c][1]) for c in (1, 2, 3)]
    for i in range(GROUP):
        rows, pair_rows = slice(i * D, (i + 1) * D), slice((i % 2) * D, (i % 2 + 1) * D)
        state = jnp.where(odd == i // 2, mine_ref[pair_rows, :], theirs_ref[pair_rows, :])
        result_ref[0, rows, :] = state
        state = state.astype(F32)
        for c in (1, 2, 3):
            state = passing[c - 1][i : i + 1] * state + ordered_ref[c - 1, rows, :].astype(F32)
            state = state * joined[c]
            result_ref[c, rows, :] = state.astype(BF16)
    for step, out_ref in enumerate((out0, out1, out2, out3)):
        out_ref[...] = result_ref[lax.rem(y + step, 4)]


def core_kernel(of_other, index, own_ref, other_ref, s0, s1, s2, s3, out_ref):
    y, core = index[Y], index[CORE]
    is_one = core == 1
    target = 1 - core if of_other else core

    @pl.when(target == 0)
    def _():
        for step, slot in enumerate((s0, s1, s2, s3)):
            out_ref[lax.rem(y + 4 - step, 4)] = slot[...]

    @pl.when(target == 1)
    def _():
        for step, slot in enumerate((s0, s1, s2, s3)):
            group = lax.rem(y + 4 - step, 4)
            decay_own, first_own, last_own = unpack_meta(own_ref[group, ROWS:PART, :])
            decay_other, first_other, last_other = unpack_meta(other_ref[group, ROWS:PART, :])
            decay = jnp.where(is_one, decay_other, decay_own)
            first0 = jnp.where(is_one, first_other, first_own)
            last0 = jnp.where(is_one, last_other, last_own)
            first1 = jnp.where(is_one, first_own, first_other)
            joined = same(last0, first1)
            passing = jnp.exp(decay) * same(first0, last0) * joined
            for i in range(GROUP):
                rows = slice(i * D, (i + 1) * D)
                earlier = jnp.where(is_one, other_ref[group, rows, :], own_ref[group, rows, :]).astype(F32)
                later = passing[i : i + 1] * slot[rows, :].astype(F32) + joined * earlier
                out_ref[group, rows, :] = later.astype(BF16)


def attend_kernel(wave, index, q_ref, intra_ref, factor_ref, mine_ref, other_ref, gain_ref, *out_refs):
    shape = (2 * GROUP, ROWS)
    spreading = (lax.rem(iota(shape, 0), GROUP) == iota(shape, 1) // D).astype(F32).astype(BF16)
    for step in range(4):
        quarter = lax.rem(index[PHASE] + step, 4)
        group = 2 * quarter + wave
        at = lax.rem(group, 4)
        use_mine = (quarter // 2) == index[CORE]
        factors = jnp.dot(factor_ref[quarter], spreading, preferred_element_type=F32)
        gain = gain_ref[group]
        for i in range(GROUP):
            lanes = slice(i * D, (i + 1) * D)
            state = jnp.where(use_mine, mine_ref[at, lanes, :], other_ref[at, lanes, :])
            queries = q_ref[:, pl.ds(pl.multiple_of(group * ROWS + i * D, D), D)]
            inter = jnp.dot(queries, state, preferred_element_type=F32)
            total = intra_ref[quarter, :, lanes] + inter * factors[:, lanes]
            power = jnp.mean(total * total, axis=1, keepdims=True)
            out_refs[step][:, lanes] = (
                total * lax.rsqrt(power + EPSILON) * gain[:, lanes].astype(F32)
            ).astype(BF16)


def attend(wave, index, *operands):
    return small_call(functools.partial(attend_kernel, wave), index, operands, [((D, ROWS), BF16)] * 4)


def layers_kernel(wave, index, tokens_ref, *refs):
    *slots, out0, out1, out2, out3, ordered_ref = refs
    phase = index[PHASE]
    in_order(phase, slots, ordered_ref)
    current = tokens_ref[:, wave * ROWS : (wave + 1) * ROWS].astype(F32)
    for s in range(4):
        rounded = (current + ordered_ref[s].astype(F32)).astype(BF16)
        ordered_ref[s] = rounded
        current = rounded.astype(F32)
    for step, out_ref in enumerate((out0, out1, out2, out3)):
        out_ref[...] = ordered_ref[lax.rem(phase + step, 4)]


def place_kernel(wave, index, *refs):
    slots, out_ref, sem = refs[:4], refs[-2], refs[-1]
    copies = []
    for step, slot in enumerate(slots):
        quarter = lax.rem(index[PHASE] + 4 - step, 4)
        lanes = pl.ds(pl.multiple_of((2 * quarter + wave) * ROWS, ROWS), ROWS)
        copies.append(pltpu.make_async_copy(slot, out_ref.at[:, lanes], sem.at[step]))
    for copy in copies:
        copy.start()
    for copy in copies:
        copy.wait()


def place(wave, index, slots, out=None):
    given = [] if out is None else [out]
    return pl.pallas_call(
        functools.partial(place_kernel, wave),
        out_shape=jax.ShapeDtypeStruct((D, HEADS * D), BF16),
        grid_spec=pltpu.PrefetchScalarGridSpec(
            num_scalar_prefetch=1,
            grid=(1,),
            in_specs=[pl.BlockSpec(memory_space=pl.ANY)] * (4 + len(given)),
            out_specs=pl.BlockSpec(memory_space=pl.ANY),
            scratch_shapes=[pltpu.SemaphoreType.DMA((4,))],
        ),
        input_output_aliases={5: 0} if given else {},
        compiler_params=pltpu.CompilerParams(vmem_limit_bytes=VMEM_LIMIT),
        cost_estimate=pl.CostEstimate(flops=0, bytes_accessed=2 * HEADS * D * D, transcendentals=0),
    )(index, *slots, *given)


def ring_exchange(slots, axis):
    size = lax.axis_size(axis)
    moved = [
        lax.ppermute(slots[d], axis, [(i, (i + d) % size) for i in range(size)]) for d in range(1, len(slots))
    ]
    return [slots[0], *moved]


def swap_rows(array):
    return lax.ppermute(array, "z", [(i, i ^ 1) for i in range(NZ)])


def swap_cores(array):
    return lax.ppermute(array, "core", [(0, 1), (1, 0)])


def local(tokens, queries, keys_in, values, norm_gain, log_decay, doc_ids):
    index = jnp.stack([lax.axis_index(name) for name in ("phase", "y", "core", "z")]).astype(jnp.int32)
    queries, keys, values, decay = queries[0, 0], keys_in[0, 0], values[0, 0], log_decay[0, 0]
    gain = norm_gain.reshape(8, 1, ROWS)

    other = swap_cores(summaries(True, index, keys, values, decay, doc_ids))
    own = summaries(False, index, keys, values, decay, doc_ids)

    part, group_states = ((PART, D), BF16), ((ROWS, D), BF16)
    slots = ring_exchange(small_call(chip_kernel, index, [own, other], [part] * 4), "y")
    intra = [intra_term(wave, queries, keys, values, decay, doc_ids) for wave in range(2)]

    pair, pair_states = ((PAIR, D), BF16), ((2 * D, D), BF16)
    send, keep = small_call(
        row_kernel,
        index,
        slots,
        [pair] * 2,
        [pltpu.VMEM((4, PART, D), BF16), pltpu.VMEM((GROUP, D, D), BF16)],
        intra[0][:1],
    )
    partner = swap_rows(send)
    (both,) = small_call(pair_kernel, index, [keep, partner], [pair])
    before = [lax.ppermute(both, "z", [(i, i + by) for i in range(NZ - by)]) for by in (2, 4, 6)]
    mine, send = small_call(prefix_kernel, index, [keep, partner, *before], [pair_states] * 2)
    spread = small_call(
        spread_kernel,
        index,
        [mine, swap_rows(send), *slots],
        [group_states] * 4,
        [pltpu.VMEM((4, PART, D), BF16), pltpu.VMEM((4, ROWS, D), BF16)],
    )
    spread = ring_exchange(spread, "y")
    for_core = lambda of_other, after: small_call(
        functools.partial(core_kernel, of_other), index, [own, other, *spread], [((4, ROWS, D), BF16)], after=after
    )[0]
    theirs = swap_cores(for_core(True, intra[1][:1]))
    mine = for_core(False, ())

    result = None
    for wave in range(2):
        normed = ring_exchange(attend(wave, index, queries, *intra[wave], mine, theirs, gain), "phase")
        sums = small_call(
            functools.partial(layers_kernel, wave),
            index,
            [tokens[0], *normed],
            [((D, ROWS), BF16)] * 4,
            [pltpu.VMEM((4, D, ROWS), BF16)],
        )
        result = place(wave, index, ring_exchange(sums, "phase"), result)
    return result[None, None]


def solution(mesh):
    grid = Mesh(mesh.devices.reshape(4, NZ, 4, 2), ("phase", "z", "y", "core"))
    ctx = ("z", "y", "core")
    rows = P("phase", None, ctx, None)
    return jax.shard_map(
        local,
        mesh=grid,
        in_specs=(
            P(None, ctx, "phase"),
            rows,
            rows,
            rows,
            P("phase", None),
            P("phase", None, None, ctx),
            P(None, ctx),
        ),
        out_specs=rows,
        check_vma=False,
    )
```

```python
import functools

import jax
import jax.numpy as jnp
from jax import lax
from jax.experimental import pallas as pl
from jax.experimental.pallas import tpu as pltpu
from jax.sharding import Mesh
from jax.sharding import PartitionSpec as P

EPSILON = 1e-05
F32, BF16 = jnp.float32, jnp.bfloat16
D = 128
HEADS = 32
HALF = HEADS // 2
GROUP = HALF // 4
NZ = 8
META = 32
ROWS = GROUP * D
PART = ROWS + META
PAIR = 2 * D + META
PHASE, Y, CORE, Z = 0, 1, 2, 3
VMEM_LIMIT = 16 * 1024 * 1024


def nt(a, b):
    return lax.dot_general(a, b, (((1,), (1,)), ((), ())), preferred_element_type=F32)


def iota(shape, axis):
    return lax.broadcasted_iota(jnp.int32, shape, axis)


def split3(x):
    hi = x.astype(BF16).astype(F32)
    mid = (x - hi).astype(BF16).astype(F32)
    return hi, mid, x - hi - mid


def three_parts(x):
    return jnp.concatenate([part.astype(BF16) for part in split3(x)], axis=1)


def running_sums(decay):
    shape = (D, 3 * D)
    lower = (lax.rem(iota(shape, 1), D) <= iota(shape, 0)).astype(F32).astype(BF16)
    return nt(three_parts(decay), lower)


def rows_of(ids_row):
    return jnp.transpose(jnp.broadcast_to(ids_row, (D, D)))


def pack_meta(decay, first, last):
    row = iota((8, D), 0)
    ids = jnp.where(row == 0, first, jnp.where(row == 1, last, 0.0))
    return jnp.concatenate([*split3(decay), ids], axis=0).astype(BF16)


def unpack_meta(meta):
    meta = meta.astype(F32)
    return meta[0:8] + meta[8:16] + meta[16:24], meta[24:25], meta[25:26]


def same(a, b):
    return (a == b).astype(F32)


def summary_kernel(of_other, index, k_ref, v_ref, decay_ref, ids_ref, out_ref, cut_ref):
    half = 1 - index[CORE] if of_other else index[CORE]
    ids = ids_ref[...].astype(F32)
    first, last = ids[:, 0:1], ids[:, D - 1 : D]
    decay = decay_ref[pl.ds(pl.multiple_of(half * HALF, HALF), HALF), :]
    total = nt(three_parts(decay), jnp.ones((D, 3 * D), BF16))
    carried = jnp.exp(total - running_sums(decay)) * same(ids, last)
    for group in range(4):
        for i in range(GROUP):
            h = group * GROUP + i
            lanes = slice(h * D, (h + 1) * D)
            keyed = (jnp.transpose(k_ref[:, lanes].astype(F32)) * carried[h : h + 1]).astype(BF16)
            state = jnp.dot(keyed, v_ref[:, lanes], preferred_element_type=F32)
            out_ref[group, i * D : (i + 1) * D, :] = state.astype(BF16)
        cut_ref[0:GROUP, :] = total[group * GROUP : (group + 1) * GROUP, :]
        cut_ref[GROUP:8, :] = jnp.zeros((8 - GROUP, D), F32)
        out_ref[group, ROWS:PART, :] = pack_meta(
            cut_ref[...], jnp.broadcast_to(first, (1, D)), jnp.broadcast_to(last, (1, D))
        )


def summaries(of_other, index, keys, values, decay, ids):
    whole = lambda shape: pl.BlockSpec(shape, lambda i, s: (0,) * len(shape))
    block = pl.BlockSpec((D, HALF * D), lambda i, s: (0, 0 if of_other else s[CORE]))
    return pl.pallas_call(
        functools.partial(summary_kernel, of_other),
        out_shape=jax.ShapeDtypeStruct((4, PART, D), BF16),
        grid_spec=pltpu.PrefetchScalarGridSpec(
            num_scalar_prefetch=1,
            grid=(1,),
            in_specs=[block, block, whole((HEADS, D)), whole((1, D))],
            out_specs=whole((4, PART, D)),
            scratch_shapes=[pltpu.VMEM((8, D), F32)],
        ),
        compiler_params=pltpu.CompilerParams(vmem_limit_bytes=VMEM_LIMIT),
        cost_estimate=pl.CostEstimate(flops=HEADS * D**3, bytes_accessed=3 * HALF * D * D * 2, transcendentals=0),
    )(index, keys, values, decay, ids)


def two_parts(x):
    hi = x.astype(BF16)
    return hi, (x - hi.astype(F32)).astype(BF16)


def intra_kernel(
    wave, q_ref, k_ref, v_ref, decay_ref, ids_ref, out_ref, factor_ref, column_ref, row_ref, allowed_ref
):
    step = pl.program_id(0)

    @pl.when(step == 0)
    def _():
        ids = ids_ref[...].astype(F32)
        row_ref[0:HEADS, :] = running_sums(decay_ref[...])
        row_ref[HEADS:D, :] = jnp.zeros((D - HEADS, D), F32)
        sums = jnp.transpose(row_ref[...])
        documents = rows_of(ids)
        scaling = jnp.exp(sums) * same(documents, ids[:, 0:1])
        for quarter in range(4):
            heads = slice(8 * quarter + GROUP * wave, 8 * quarter + GROUP * (wave + 1))
            column_ref[quarter, :, 0:GROUP] = sums[:, heads]
            factor_ref[quarter] = jnp.concatenate(two_parts(scaling[:, heads]), axis=1)
        allowed_ref[...] = ((iota((D, D), 1) <= iota((D, D), 0)) & (documents == ids)).astype(F32)

    allowed = allowed_ref[...] > 0.0
    columns = column_ref[step]
    rows = row_ref[pl.ds(pl.multiple_of(8 * step, 8), 8), :]
    for i in range(GROUP):
        h = GROUP * wave + i
        lanes = slice(i * D, (i + 1) * D)
        spread = jnp.minimum(columns[:, i : i + 1] - rows[h : h + 1, :], 0.0)
        weighting = jnp.where(allowed, jnp.exp(spread), 0.0)
        keys = jnp.transpose(k_ref[:, lanes].astype(F32)).astype(BF16)
        attn = (jnp.dot(q_ref[:, lanes], keys, preferred_element_type=F32) * weighting).astype(BF16)
        out_ref[0, :, lanes] = jnp.dot(attn, v_ref[:, lanes], preferred_element_type=F32)


def intra_term(wave, queries, keys, values, decay, ids):
    block = pl.BlockSpec((D, ROWS), lambda i: (0, 2 * i + wave))
    return pl.pallas_call(
        functools.partial(intra_kernel, wave),
        out_shape=[jax.ShapeDtypeStruct((4, D, ROWS), F32), jax.ShapeDtypeStruct((4, D, 2 * GROUP), BF16)],
        grid=(4,),
        in_specs=[
            block,
            block,
            block,
            pl.BlockSpec((HEADS, D), lambda i: (0, 0)),
            pl.BlockSpec((1, D), lambda i: (0, 0)),
        ],
        out_specs=[
            pl.BlockSpec((1, D, ROWS), lambda i: (i, 0, 0)),
            pl.BlockSpec((4, D, 2 * GROUP), lambda i: (0, 0, 0)),
        ],
        scratch_shapes=[pltpu.VMEM((4, D, 8), F32), pltpu.VMEM((D, D), F32), pltpu.VMEM((D, D), F32)],
        compiler_params=pltpu.CompilerParams(vmem_limit_bytes=VMEM_LIMIT),
        cost_estimate=pl.CostEstimate(
            flops=2 * HEADS * D**3, bytes_accessed=5 * HALF * D * D * 2, transcendentals=HALF * D * D
        ),
    )(queries, keys, values, decay, ids)


def chip_kernel(index, own_ref, other_ref, *out_refs):
    y, core = index[Y], index[CORE]
    is_one = core == 1
    for step in range(4):
        group = lax.rem(y + step, 4)
        decay_own, first_own, last_own = unpack_meta(own_ref[group, ROWS:PART, :])
        decay_other, first_other, last_other = unpack_meta(other_ref[group, ROWS:PART, :])
        joined = same(last_own, last_other)
        later = jnp.where(is_one, decay_own, decay_other)
        passed = jnp.exp(later) * joined
        weight_own = jnp.where(is_one, 1.0, passed)
        weight_other = jnp.where(is_one, passed, 1.0)
        for i in range(GROUP):
            rows = slice(i * D, (i + 1) * D)
            out_refs[step][rows, :] = (
                weight_own[i : i + 1] * own_ref[group, rows, :].astype(F32)
                + weight_other[i : i + 1] * other_ref[group, rows, :].astype(F32)
            ).astype(BF16)
        out_refs[step][ROWS:PART, :] = pack_meta(
            decay_own + decay_other,
            jnp.where(is_one, first_other, first_own),
            jnp.where(is_one, last_own, last_other),
        )


def small_call(kernel, index, operands, outs, scratch=(), after=()):
    whole = lambda shape: pl.BlockSpec(shape, lambda i, s: (0,) * len(shape))
    size = sum(a.size * a.dtype.itemsize for a in operands)
    many, extra = len(operands), len(after)

    def body(index, *refs):
        kernel(index, *refs[:many], *refs[many + extra :])

    return pl.pallas_call(
        body,
        out_shape=[jax.ShapeDtypeStruct(shape, dtype) for shape, dtype in outs],
        grid_spec=pltpu.PrefetchScalarGridSpec(
            num_scalar_prefetch=1,
            grid=(1,),
            in_specs=[whole(a.shape) for a in operands] + [pl.BlockSpec(memory_space=pl.ANY)] * extra,
            out_specs=[whole(shape) for shape, _ in outs],
            scratch_shapes=list(scratch),
        ),
        compiler_params=pltpu.CompilerParams(vmem_limit_bytes=VMEM_LIMIT),
        cost_estimate=pl.CostEstimate(flops=size, bytes_accessed=2 * size, transcendentals=0),
    )(index, *operands, *after)


def in_order(y, slots, ordered_ref):
    for step in range(4):
        ordered_ref[lax.rem(y + 4 - step, 4)] = slots[step][...]


def row_kernel(index, *refs):
    *slots, send_ref, keep_ref, ordered_ref, state_ref = refs
    in_order(index[Y], slots, ordered_ref)
    metas = [unpack_meta(ordered_ref[c, ROWS:PART, :]) for c in range(4)]
    weights, after = [None] * 4, jnp.zeros((8, D), F32)
    for c in (3, 2, 1, 0):
        weights[c] = jnp.exp(after) * same(metas[c][2], metas[3][2])
        after = after + metas[c][0]
    for i in range(GROUP):
        rows = slice(i * D, (i + 1) * D)
        state = sum(weights[c][i : i + 1] * ordered_ref[c, rows, :].astype(F32) for c in range(4))
        state_ref[i] = state.astype(BF16)
    odd = lax.rem(index[Z], 2)
    turned = jnp.concatenate([after[2:4], after[0:2], after[4:8]], axis=0)
    for out_ref, half in ((send_ref, 1 - odd), (keep_ref, odd)):
        for i in range(2):
            out_ref[i * D : (i + 1) * D, :] = state_ref[2 * half + i]
        out_ref[2 * D : PAIR, :] = pack_meta(jnp.where(half == 0, after, turned), metas[0][1], metas[3][2])


def pair_kernel(index, own_ref, other_ref, out_ref):
    is_odd = lax.rem(index[Z], 2) == 1
    decay_own, first_own, last_own = unpack_meta(own_ref[2 * D : PAIR, :])
    decay_other, first_other, last_other = unpack_meta(other_ref[2 * D : PAIR, :])
    passed = jnp.exp(jnp.where(is_odd, decay_own, decay_other)) * same(last_own, last_other)
    weight_own = jnp.where(is_odd, 1.0, passed)
    weight_other = jnp.where(is_odd, passed, 1.0)
    for i in range(2):
        rows = slice(i * D, (i + 1) * D)
        out_ref[rows, :] = (
            weight_own[i : i + 1] * own_ref[rows, :].astype(F32)
            + weight_other[i : i + 1] * other_ref[rows, :].astype(F32)
        ).astype(BF16)
    out_ref[2 * D : PAIR, :] = pack_meta(
        decay_own + decay_other,
        jnp.where(is_odd, first_other, first_own),
        jnp.where(is_odd, last_own, last_other),
    )


def prefix_kernel(index, own_ref, other_ref, *refs):
    *before, mine_ref, send_ref = refs
    is_odd = lax.rem(index[Z], 2) == 1
    decay_own, first_own, last_own = unpack_meta(own_ref[2 * D : PAIR, :])
    decay_other, first_other, last_other = unpack_meta(other_ref[2 * D : PAIR, :])
    decay0 = jnp.where(is_odd, decay_other, decay_own)
    first0, first1 = jnp.where(is_odd, first_other, first_own), jnp.where(is_odd, first_own, first_other)
    last0 = jnp.where(is_odd, last_other, last_own)
    joined = same(last0, first1)
    passing = jnp.exp(decay0) * same(first0, last0) * joined
    weights, after = [], jnp.zeros((8, D), F32)
    for back, pair in enumerate(before, start=1):
        decay, _, last = unpack_meta(pair[2 * D : PAIR, :])
        weights.append(jnp.where(index[Z] >= 2 * back, jnp.exp(after) * same(last, first0), 0.0))
        after = after + decay
    for i in range(2):
        rows = slice(i * D, (i + 1) * D)
        state = sum(w[i : i + 1] * pair[rows, :].astype(F32) for w, pair in zip(weights, before))
        earlier = jnp.where(is_odd, other_ref[rows, :], own_ref[rows, :]).astype(F32)
        later = passing[i : i + 1] * state + joined * earlier
        mine_ref[rows, :] = jnp.where(is_odd, later, state).astype(BF16)
        send_ref[rows, :] = jnp.where(is_odd, state, later).astype(BF16)


def spread_kernel(index, mine_ref, theirs_ref, *refs):
    *slots, out0, out1, out2, out3, ordered_ref, result_ref = refs
    y, odd = index[Y], lax.rem(index[Z], 2)
    in_order(y, slots, ordered_ref)
    metas = [unpack_meta(ordered_ref[c, ROWS:PART, :]) for c in range(4)]
    passing = [jnp.exp(decay) * same(first, last) for decay, first, last in metas]
    joined = [None] + [same(metas[c - 1][2], metas[c][1]) for c in (1, 2, 3)]
    for i in range(GROUP):
        rows, pair_rows = slice(i * D, (i + 1) * D), slice((i % 2) * D, (i % 2 + 1) * D)
        state = jnp.where(odd == i // 2, mine_ref[pair_rows, :], theirs_ref[pair_rows, :])
        result_ref[0, rows, :] = state
        state = state.astype(F32)
        for c in (1, 2, 3):
            state = passing[c - 1][i : i + 1] * state + ordered_ref[c - 1, rows, :].astype(F32)
            state = state * joined[c]
            result_ref[c, rows, :] = state.astype(BF16)
    for step, out_ref in enumerate((out0, out1, out2, out3)):
        out_ref[...] = result_ref[lax.rem(y + step, 4)]


def core_kernel(of_other, index, own_ref, other_ref, s0, s1, s2, s3, out_ref):
    y, core = index[Y], index[CORE]
    is_one = core == 1
    target = 1 - core if of_other else core

    @pl.when(target == 0)
    def _():
        for step, slot in enumerate((s0, s1, s2, s3)):
            out_ref[lax.rem(y + 4 - step, 4)] = slot[...]

    @pl.when(target == 1)
    def _():
        for step, slot in enumerate((s0, s1, s2, s3)):
            group = lax.rem(y + 4 - step, 4)
            decay_own, first_own, last_own = unpack_meta(own_ref[group, ROWS:PART, :])
            decay_other, first_other, last_other = unpack_meta(other_ref[group, ROWS:PART, :])
            decay = jnp.where(is_one, decay_other, decay_own)
            first0 = jnp.where(is_one, first_other, first_own)
            last0 = jnp.where(is_one, last_other, last_own)
            first1 = jnp.where(is_one, first_own, first_other)
            joined = same(last0, first1)
            passing = jnp.exp(decay) * same(first0, last0) * joined
            for i in range(GROUP):
                rows = slice(i * D, (i + 1) * D)
                earlier = jnp.where(is_one, other_ref[group, rows, :], own_ref[group, rows, :]).astype(F32)
                later = passing[i : i + 1] * slot[rows, :].astype(F32) + joined * earlier
                out_ref[group, rows, :] = later.astype(BF16)


def attend_kernel(wave, index, q_ref, intra_ref, factor_ref, mine_ref, other_ref, gain_ref, *out_refs):
    shape = (2 * GROUP, ROWS)
    spreading = (lax.rem(iota(shape, 0), GROUP) == iota(shape, 1) // D).astype(F32).astype(BF16)
    for step in range(4):
        quarter = lax.rem(index[PHASE] + step, 4)
        group = 2 * quarter + wave
        at = lax.rem(group, 4)
        use_mine = (quarter // 2) == index[CORE]
        factors = jnp.dot(factor_ref[quarter], spreading, preferred_element_type=F32)
        gain = gain_ref[group]
        for i in range(GROUP):
            lanes = slice(i * D, (i + 1) * D)
            state = jnp.where(use_mine, mine_ref[at, lanes, :], other_ref[at, lanes, :])
            queries = q_ref[:, pl.ds(pl.multiple_of(group * ROWS + i * D, D), D)]
            inter = jnp.dot(queries, state, preferred_element_type=F32)
            total = intra_ref[quarter, :, lanes] + inter * factors[:, lanes]
            power = jnp.mean(total * total, axis=1, keepdims=True)
            out_refs[step][:, lanes] = (
                total * lax.rsqrt(power + EPSILON) * gain[:, lanes].astype(F32)
            ).astype(BF16)


def attend(wave, index, *operands):
    return small_call(functools.partial(attend_kernel, wave), index, operands, [((D, ROWS), BF16)] * 4)


def layers_kernel(wave, index, tokens_ref, *refs):
    *slots, out0, out1, out2, out3, ordered_ref = refs
    phase = index[PHASE]
    in_order(phase, slots, ordered_ref)
    current = tokens_ref[:, wave * ROWS : (wave + 1) * ROWS].astype(F32)
    for s in range(4):
        rounded = (current + ordered_ref[s].astype(F32)).astype(BF16)
        ordered_ref[s] = rounded
        current = rounded.astype(F32)
    for step, out_ref in enumerate((out0, out1, out2, out3)):
        out_ref[...] = ordered_ref[lax.rem(phase + step, 4)]


def place_kernel(wave, index, *refs):
    slots, out_ref, sem = refs[:4], refs[-2], refs[-1]
    copies = []
    for step, slot in enumerate(slots):
        quarter = lax.rem(index[PHASE] + 4 - step, 4)
        lanes = pl.ds(pl.multiple_of((2 * quarter + wave) * ROWS, ROWS), ROWS)
        copies.append(pltpu.make_async_copy(slot, out_ref.at[:, lanes], sem.at[step]))
    for copy in copies:
        copy.start()
    for copy in copies:
        copy.wait()


def place(wave, index, slots, out=None):
    given = [] if out is None else [out]
    return pl.pallas_call(
        functools.partial(place_kernel, wave),
        out_shape=jax.ShapeDtypeStruct((D, HEADS * D), BF16),
        grid_spec=pltpu.PrefetchScalarGridSpec(
            num_scalar_prefetch=1,
            grid=(1,),
            in_specs=[pl.BlockSpec(memory_space=pl.ANY)] * (4 + len(given)),
            out_specs=pl.BlockSpec(memory_space=pl.ANY),
            scratch_shapes=[pltpu.SemaphoreType.DMA((4,))],
        ),
        input_output_aliases={5: 0} if given else {},
        compiler_params=pltpu.CompilerParams(vmem_limit_bytes=VMEM_LIMIT),
        cost_estimate=pl.CostEstimate(flops=0, bytes_accessed=2 * HEADS * D * D, transcendentals=0),
    )(index, *slots, *given)


def ring_exchange(slots, axis):
    size = lax.axis_size(axis)
    moved = [
        lax.ppermute(slots[d], axis, [(i, (i + d) % size) for i in range(size)]) for d in range(1, len(slots))
    ]
    return [slots[0], *moved]


def swap_rows(array):
    return lax.ppermute(array, "z", [(i, i ^ 1) for i in range(NZ)])


def swap_cores(array):
    return lax.ppermute(array, "core", [(0, 1), (1, 0)])


def local(tokens, queries, keys_in, values, norm_gain, log_decay, doc_ids):
    index = jnp.stack([lax.axis_index(name) for name in ("phase", "y", "core", "z")]).astype(jnp.int32)
    queries, keys, values, decay = queries[0, 0], keys_in[0, 0], values[0, 0], log_decay[0, 0]
    gain = norm_gain.reshape(8, 1, ROWS)

    others_lanes = (1 - index[CORE]) * HALF * D
    others = [lax.dynamic_slice_in_dim(array, others_lanes, HALF * D, 1) for array in (keys, values)]
    other = swap_cores(summaries(True, index, *others, decay, doc_ids))
    own = summaries(False, index, keys, values, decay, doc_ids)

    part, group_states = ((PART, D), BF16), ((ROWS, D), BF16)
    slots = ring_exchange(small_call(chip_kernel, index, [own, other], [part] * 4), "y")
    intra = [intra_term(wave, queries, keys, values, decay, doc_ids) for wave in range(2)]

    pair, pair_states = ((PAIR, D), BF16), ((2 * D, D), BF16)
    send, keep = small_call(
        row_kernel,
        index,
        slots,
        [pair] * 2,
        [pltpu.VMEM((4, PART, D), BF16), pltpu.VMEM((GROUP, D, D), BF16)],
        intra[0][:1],
    )
    partner = swap_rows(send)
    (both,) = small_call(pair_kernel, index, [keep, partner], [pair])
    before = [lax.ppermute(both, "z", [(i, (i + by) % NZ) for i in range(NZ)]) for by in (2, 4, 6)]
    mine, send = small_call(prefix_kernel, index, [keep, partner, *before], [pair_states] * 2)
    spread = small_call(
        spread_kernel,
        index,
        [mine, swap_rows(send), *slots],
        [group_states] * 4,
        [pltpu.VMEM((4, PART, D), BF16), pltpu.VMEM((4, ROWS, D), BF16)],
    )
    spread = ring_exchange(spread, "y")
    for_core = lambda of_other, after: small_call(
        functools.partial(core_kernel, of_other), index, [own, other, *spread], [((4, ROWS, D), BF16)], after=after
    )[0]
    theirs = swap_cores(for_core(True, intra[1][:1]))
    mine = for_core(False, ())

    result = None
    for wave in range(2):
        normed = ring_exchange(attend(wave, index, queries, *intra[wave], mine, theirs, gain), "phase")
        sums = small_call(
            functools.partial(layers_kernel, wave),
            index,
            [tokens[0], *normed],
            [((D, ROWS), BF16)] * 4,
            [pltpu.VMEM((4, D, ROWS), BF16)],
        )
        result = place(wave, index, ring_exchange(sums, "phase"), result)
    return result[None, None]


def solution(mesh):
    grid = Mesh(mesh.devices.reshape(4, NZ, 4, 2), ("phase", "z", "y", "core"))
    ctx = ("z", "y", "core")
    rows = P("phase", None, ctx, None)
    return jax.shard_map(
        local,
        mesh=grid,
        in_specs=(
            P(None, ctx, "phase"),
            rows,
            rows,
            rows,
            P("phase", None),
            P("phase", None, None, ctx),
            P(None, ctx),
        ),
        out_specs=rows,
        check_vma=False,
    )
```

```python
import functools

import jax
import jax.numpy as jnp
from jax import lax
from jax.experimental import pallas as pl
from jax.experimental.pallas import tpu as pltpu
from jax.sharding import Mesh
from jax.sharding import PartitionSpec as P

EPSILON = 1e-05
F32, BF16 = jnp.float32, jnp.bfloat16
D = 128
HEADS = 32
HALF = HEADS // 2
GROUP = HALF // 4
NZ = 8
META = 32
ROWS = GROUP * D
PART = ROWS + META
PAIR = 2 * D + META
PHASE, Y, CORE, Z = 0, 1, 2, 3
VMEM_LIMIT = 16 * 1024 * 1024


def nt(a, b):
    return lax.dot_general(a, b, (((1,), (1,)), ((), ())), preferred_element_type=F32)


def iota(shape, axis):
    return lax.broadcasted_iota(jnp.int32, shape, axis)


def split3(x):
    hi = x.astype(BF16).astype(F32)
    mid = (x - hi).astype(BF16).astype(F32)
    return hi, mid, x - hi - mid


def three_parts(x):
    return jnp.concatenate([part.astype(BF16) for part in split3(x)], axis=1)


def running_sums(decay):
    shape = (D, 3 * D)
    lower = (lax.rem(iota(shape, 1), D) <= iota(shape, 0)).astype(F32).astype(BF16)
    return nt(three_parts(decay), lower)


def rows_of(ids_row):
    return jnp.transpose(jnp.broadcast_to(ids_row, (D, D)))


def pack_meta(decay, first, last):
    row = iota((8, D), 0)
    ids = jnp.where(row == 0, first, jnp.where(row == 1, last, 0.0))
    return jnp.concatenate([*split3(decay), ids], axis=0).astype(BF16)


def unpack_meta(meta):
    meta = meta.astype(F32)
    return meta[0:8] + meta[8:16] + meta[16:24], meta[24:25], meta[25:26]


def same(a, b):
    return (a == b).astype(F32)


def summary_kernel(of_other, index, k_ref, v_ref, decay_ref, ids_ref, out_ref, cut_ref):
    half = 1 - index[CORE] if of_other else index[CORE]
    ids = ids_ref[...].astype(F32)
    first, last = ids[:, 0:1], ids[:, D - 1 : D]
    decay = decay_ref[pl.ds(pl.multiple_of(half * HALF, HALF), HALF), :]
    total = nt(three_parts(decay), jnp.ones((D, 3 * D), BF16))
    carried = jnp.exp(total - running_sums(decay)) * same(ids, last)
    for group in range(4):
        group_lanes = slice(group * ROWS, (group + 1) * ROWS)
        keys, values = k_ref[:, group_lanes], v_ref[:, group_lanes]
        for i in range(GROUP):
            h = group * GROUP + i
            lanes = slice(i * D, (i + 1) * D)
            keyed = (jnp.transpose(keys[:, lanes].astype(F32)) * carried[h : h + 1]).astype(BF16)
            state = jnp.dot(keyed, values[:, lanes], preferred_element_type=F32)
            out_ref[group, i * D : (i + 1) * D, :] = state.astype(BF16)
        cut_ref[0:GROUP, :] = total[group * GROUP : (group + 1) * GROUP, :]
        cut_ref[GROUP:8, :] = jnp.zeros((8 - GROUP, D), F32)
        out_ref[group, ROWS:PART, :] = pack_meta(
            cut_ref[...], jnp.broadcast_to(first, (1, D)), jnp.broadcast_to(last, (1, D))
        )


def summaries(of_other, index, keys, values, decay, ids):
    whole = lambda shape: pl.BlockSpec(shape, lambda i, s: (0,) * len(shape))
    block = pl.BlockSpec((D, HALF * D), lambda i, s: (0, 0 if of_other else s[CORE]))
    return pl.pallas_call(
        functools.partial(summary_kernel, of_other),
        out_shape=jax.ShapeDtypeStruct((4, PART, D), BF16),
        grid_spec=pltpu.PrefetchScalarGridSpec(
            num_scalar_prefetch=1,
            grid=(1,),
            in_specs=[block, block, whole((HEADS, D)), whole((1, D))],
            out_specs=whole((4, PART, D)),
            scratch_shapes=[pltpu.VMEM((8, D), F32)],
        ),
        compiler_params=pltpu.CompilerParams(vmem_limit_bytes=VMEM_LIMIT),
        cost_estimate=pl.CostEstimate(flops=HEADS * D**3, bytes_accessed=3 * HALF * D * D * 2, transcendentals=0),
    )(index, keys, values, decay, ids)


def two_parts(x):
    hi = x.astype(BF16)
    return hi, (x - hi.astype(F32)).astype(BF16)


def intra_kernel(
    wave, q_ref, k_ref, v_ref, decay_ref, ids_ref, out_ref, factor_ref, column_ref, row_ref, allowed_ref
):
    step = pl.program_id(0)

    @pl.when(step == 0)
    def _():
        ids = ids_ref[...].astype(F32)
        row_ref[0:HEADS, :] = running_sums(decay_ref[...])
        row_ref[HEADS:D, :] = jnp.zeros((D - HEADS, D), F32)
        sums = jnp.transpose(row_ref[...])
        documents = rows_of(ids)
        scaling = jnp.exp(sums) * same(documents, ids[:, 0:1])
        for quarter in range(4):
            heads = slice(8 * quarter + GROUP * wave, 8 * quarter + GROUP * (wave + 1))
            column_ref[quarter, :, 0:GROUP] = sums[:, heads]
            factor_ref[quarter] = jnp.concatenate(two_parts(scaling[:, heads]), axis=1)
        allowed_ref[...] = ((iota((D, D), 1) <= iota((D, D), 0)) & (documents == ids)).astype(F32)

    allowed = allowed_ref[...] > 0.0
    columns = column_ref[step]
    rows = row_ref[pl.ds(pl.multiple_of(8 * step, 8), 8), :]
    for i in range(GROUP):
        h = GROUP * wave + i
        lanes = slice(i * D, (i + 1) * D)
        spread = jnp.minimum(columns[:, i : i + 1] - rows[h : h + 1, :], 0.0)
        weighting = jnp.where(allowed, jnp.exp(spread), 0.0)
        keys = jnp.transpose(k_ref[:, lanes].astype(F32)).astype(BF16)
        attn = (jnp.dot(q_ref[:, lanes], keys, preferred_element_type=F32) * weighting).astype(BF16)
        out_ref[0, :, lanes] = jnp.dot(attn, v_ref[:, lanes], preferred_element_type=F32)


def intra_term(wave, queries, keys, values, decay, ids):
    block = pl.BlockSpec((D, ROWS), lambda i: (0, 2 * i + wave))
    return pl.pallas_call(
        functools.partial(intra_kernel, wave),
        out_shape=[jax.ShapeDtypeStruct((4, D, ROWS), F32), jax.ShapeDtypeStruct((4, D, 2 * GROUP), BF16)],
        grid=(4,),
        in_specs=[
            block,
            block,
            block,
            pl.BlockSpec((HEADS, D), lambda i: (0, 0)),
            pl.BlockSpec((1, D), lambda i: (0, 0)),
        ],
        out_specs=[
            pl.BlockSpec((1, D, ROWS), lambda i: (i, 0, 0)),
            pl.BlockSpec((4, D, 2 * GROUP), lambda i: (0, 0, 0)),
        ],
        scratch_shapes=[pltpu.VMEM((4, D, 8), F32), pltpu.VMEM((D, D), F32), pltpu.VMEM((D, D), F32)],
        compiler_params=pltpu.CompilerParams(vmem_limit_bytes=VMEM_LIMIT),
        cost_estimate=pl.CostEstimate(
            flops=2 * HEADS * D**3, bytes_accessed=5 * HALF * D * D * 2, transcendentals=HALF * D * D
        ),
    )(queries, keys, values, decay, ids)


def chip_kernel(index, own_ref, other_ref, *out_refs):
    y, core = index[Y], index[CORE]
    is_one = core == 1
    for step in range(4):
        group = lax.rem(y + step, 4)
        decay_own, first_own, last_own = unpack_meta(own_ref[group, ROWS:PART, :])
        decay_other, first_other, last_other = unpack_meta(other_ref[group, ROWS:PART, :])
        joined = same(last_own, last_other)
        later = jnp.where(is_one, decay_own, decay_other)
        passed = jnp.exp(later) * joined
        weight_own = jnp.where(is_one, 1.0, passed)
        weight_other = jnp.where(is_one, passed, 1.0)
        for i in range(GROUP):
            rows = slice(i * D, (i + 1) * D)
            out_refs[step][rows, :] = (
                weight_own[i : i + 1] * own_ref[group, rows, :].astype(F32)
                + weight_other[i : i + 1] * other_ref[group, rows, :].astype(F32)
            ).astype(BF16)
        out_refs[step][ROWS:PART, :] = pack_meta(
            decay_own + decay_other,
            jnp.where(is_one, first_other, first_own),
            jnp.where(is_one, last_own, last_other),
        )


def small_call(kernel, index, operands, outs, scratch=(), after=()):
    whole = lambda shape: pl.BlockSpec(shape, lambda i, s: (0,) * len(shape))
    size = sum(a.size * a.dtype.itemsize for a in operands)
    many, extra = len(operands), len(after)

    def body(index, *refs):
        kernel(index, *refs[:many], *refs[many + extra :])

    return pl.pallas_call(
        body,
        out_shape=[jax.ShapeDtypeStruct(shape, dtype) for shape, dtype in outs],
        grid_spec=pltpu.PrefetchScalarGridSpec(
            num_scalar_prefetch=1,
            grid=(1,),
            in_specs=[whole(a.shape) for a in operands] + [pl.BlockSpec(memory_space=pl.ANY)] * extra,
            out_specs=[whole(shape) for shape, _ in outs],
            scratch_shapes=list(scratch),
        ),
        compiler_params=pltpu.CompilerParams(vmem_limit_bytes=VMEM_LIMIT),
        cost_estimate=pl.CostEstimate(flops=size, bytes_accessed=2 * size, transcendentals=0),
    )(index, *operands, *after)


def in_order(y, slots, ordered_ref):
    for step in range(4):
        ordered_ref[lax.rem(y + 4 - step, 4)] = slots[step][...]


def row_kernel(index, *refs):
    *slots, send_ref, keep_ref, ordered_ref, state_ref = refs
    in_order(index[Y], slots, ordered_ref)
    metas = [unpack_meta(ordered_ref[c, ROWS:PART, :]) for c in range(4)]
    weights, after = [None] * 4, jnp.zeros((8, D), F32)
    for c in (3, 2, 1, 0):
        weights[c] = jnp.exp(after) * same(metas[c][2], metas[3][2])
        after = after + metas[c][0]
    for i in range(GROUP):
        rows = slice(i * D, (i + 1) * D)
        state = sum(weights[c][i : i + 1] * ordered_ref[c, rows, :].astype(F32) for c in range(4))
        state_ref[i] = state.astype(BF16)
    odd = lax.rem(index[Z], 2)
    turned = jnp.concatenate([after[2:4], after[0:2], after[4:8]], axis=0)
    for out_ref, half in ((send_ref, 1 - odd), (keep_ref, odd)):
        for i in range(2):
            out_ref[i * D : (i + 1) * D, :] = state_ref[2 * half + i]
        out_ref[2 * D : PAIR, :] = pack_meta(jnp.where(half == 0, after, turned), metas[0][1], metas[3][2])


def pair_kernel(index, own_ref, other_ref, out_ref):
    is_odd = lax.rem(index[Z], 2) == 1
    decay_own, first_own, last_own = unpack_meta(own_ref[2 * D : PAIR, :])
    decay_other, first_other, last_other = unpack_meta(other_ref[2 * D : PAIR, :])
    passed = jnp.exp(jnp.where(is_odd, decay_own, decay_other)) * same(last_own, last_other)
    weight_own = jnp.where(is_odd, 1.0, passed)
    weight_other = jnp.where(is_odd, passed, 1.0)
    for i in range(2):
        rows = slice(i * D, (i + 1) * D)
        out_ref[rows, :] = (
            weight_own[i : i + 1] * own_ref[rows, :].astype(F32)
            + weight_other[i : i + 1] * other_ref[rows, :].astype(F32)
        ).astype(BF16)
    out_ref[2 * D : PAIR, :] = pack_meta(
        decay_own + decay_other,
        jnp.where(is_odd, first_other, first_own),
        jnp.where(is_odd, last_own, last_other),
    )


def prefix_kernel(index, own_ref, other_ref, *refs):
    *before, mine_ref, send_ref = refs
    is_odd = lax.rem(index[Z], 2) == 1
    decay_own, first_own, last_own = unpack_meta(own_ref[2 * D : PAIR, :])
    decay_other, first_other, last_other = unpack_meta(other_ref[2 * D : PAIR, :])
    decay0 = jnp.where(is_odd, decay_other, decay_own)
    first0, first1 = jnp.where(is_odd, first_other, first_own), jnp.where(is_odd, first_own, first_other)
    last0 = jnp.where(is_odd, last_other, last_own)
    joined = same(last0, first1)
    passing = jnp.exp(decay0) * same(first0, last0) * joined
    weights, after = [], jnp.zeros((8, D), F32)
    for back, pair in enumerate(before, start=1):
        decay, _, last = unpack_meta(pair[2 * D : PAIR, :])
        weights.append(jnp.where(index[Z] >= 2 * back, jnp.exp(after) * same(last, first0), 0.0))
        after = after + decay
    for i in range(2):
        rows = slice(i * D, (i + 1) * D)
        state = sum(w[i : i + 1] * pair[rows, :].astype(F32) for w, pair in zip(weights, before))
        earlier = jnp.where(is_odd, other_ref[rows, :], own_ref[rows, :]).astype(F32)
        later = passing[i : i + 1] * state + joined * earlier
        mine_ref[rows, :] = jnp.where(is_odd, later, state).astype(BF16)
        send_ref[rows, :] = jnp.where(is_odd, state, later).astype(BF16)


def spread_kernel(index, mine_ref, theirs_ref, *refs):
    *slots, out0, out1, out2, out3, ordered_ref, result_ref = refs
    y, odd = index[Y], lax.rem(index[Z], 2)
    in_order(y, slots, ordered_ref)
    metas = [unpack_meta(ordered_ref[c, ROWS:PART, :]) for c in range(4)]
    passing = [jnp.exp(decay) * same(first, last) for decay, first, last in metas]
    joined = [None] + [same(metas[c - 1][2], metas[c][1]) for c in (1, 2, 3)]
    for i in range(GROUP):
        rows, pair_rows = slice(i * D, (i + 1) * D), slice((i % 2) * D, (i % 2 + 1) * D)
        state = jnp.where(odd == i // 2, mine_ref[pair_rows, :], theirs_ref[pair_rows, :])
        result_ref[0, rows, :] = state
        state = state.astype(F32)
        for c in (1, 2, 3):
            state = passing[c - 1][i : i + 1] * state + ordered_ref[c - 1, rows, :].astype(F32)
            state = state * joined[c]
            result_ref[c, rows, :] = state.astype(BF16)
    for step, out_ref in enumerate((out0, out1, out2, out3)):
        out_ref[...] = result_ref[lax.rem(y + step, 4)]


def core_kernel(of_other, index, own_ref, other_ref, s0, s1, s2, s3, out_ref):
    y, core = index[Y], index[CORE]
    is_one = core == 1
    target = 1 - core if of_other else core

    @pl.when(target == 0)
    def _():
        for step, slot in enumerate((s0, s1, s2, s3)):
            out_ref[lax.rem(y + 4 - step, 4)] = slot[...]

    @pl.when(target == 1)
    def _():
        for step, slot in enumerate((s0, s1, s2, s3)):
            group = lax.rem(y + 4 - step, 4)
            decay_own, first_own, last_own = unpack_meta(own_ref[group, ROWS:PART, :])
            decay_other, first_other, last_other = unpack_meta(other_ref[group, ROWS:PART, :])
            decay = jnp.where(is_one, decay_other, decay_own)
            first0 = jnp.where(is_one, first_other, first_own)
            last0 = jnp.where(is_one, last_other, last_own)
            first1 = jnp.where(is_one, first_own, first_other)
            joined = same(last0, first1)
            passing = jnp.exp(decay) * same(first0, last0) * joined
            for i in range(GROUP):
                rows = slice(i * D, (i + 1) * D)
                earlier = jnp.where(is_one, other_ref[group, rows, :], own_ref[group, rows, :]).astype(F32)
                later = passing[i : i + 1] * slot[rows, :].astype(F32) + joined * earlier
                out_ref[group, rows, :] = later.astype(BF16)


def attend_kernel(wave, index, q_ref, intra_ref, factor_ref, mine_ref, other_ref, gain_ref, *out_refs):
    shape = (2 * GROUP, ROWS)
    spreading = (lax.rem(iota(shape, 0), GROUP) == iota(shape, 1) // D).astype(F32).astype(BF16)
    for step in range(4):
        quarter = lax.rem(index[PHASE] + step, 4)
        group = 2 * quarter + wave
        at = lax.rem(group, 4)
        use_mine = (quarter // 2) == index[CORE]
        factors = jnp.dot(factor_ref[quarter], spreading, preferred_element_type=F32)
        gain = gain_ref[group]
        for i in range(GROUP):
            lanes = slice(i * D, (i + 1) * D)
            state = jnp.where(use_mine, mine_ref[at, lanes, :], other_ref[at, lanes, :])
            queries = q_ref[:, pl.ds(pl.multiple_of(group * ROWS + i * D, D), D)]
            inter = jnp.dot(queries, state, preferred_element_type=F32)
            total = intra_ref[quarter, :, lanes] + inter * factors[:, lanes]
            power = jnp.mean(total * total, axis=1, keepdims=True)
            out_refs[step][:, lanes] = (
                total * lax.rsqrt(power + EPSILON) * gain[:, lanes].astype(F32)
            ).astype(BF16)


def attend(wave, index, *operands):
    return small_call(functools.partial(attend_kernel, wave), index, operands, [((D, ROWS), BF16)] * 4)


def layers_kernel(wave, index, tokens_ref, *refs):
    *slots, out0, out1, out2, out3, ordered_ref = refs
    phase = index[PHASE]
    in_order(phase, slots, ordered_ref)
    current = tokens_ref[:, wave * ROWS : (wave + 1) * ROWS].astype(F32)
    for s in range(4):
        rounded = (current + ordered_ref[s].astype(F32)).astype(BF16)
        ordered_ref[s] = rounded
        current = rounded.astype(F32)
    for step, out_ref in enumerate((out0, out1, out2, out3)):
        out_ref[...] = ordered_ref[lax.rem(phase + step, 4)]


def place_kernel(wave, index, *refs):
    slots, out_ref, sem = refs[:4], refs[-2], refs[-1]
    copies = []
    for step, slot in enumerate(slots):
        quarter = lax.rem(index[PHASE] + 4 - step, 4)
        lanes = pl.ds(pl.multiple_of((2 * quarter + wave) * ROWS, ROWS), ROWS)
        copies.append(pltpu.make_async_copy(slot, out_ref.at[:, lanes], sem.at[step]))
    for copy in copies:
        copy.start()
    for copy in copies:
        copy.wait()


def place(wave, index, slots, out=None):
    given = [] if out is None else [out]
    return pl.pallas_call(
        functools.partial(place_kernel, wave),
        out_shape=jax.ShapeDtypeStruct((D, HEADS * D), BF16),
        grid_spec=pltpu.PrefetchScalarGridSpec(
            num_scalar_prefetch=1,
            grid=(1,),
            in_specs=[pl.BlockSpec(memory_space=pl.ANY)] * (4 + len(given)),
            out_specs=pl.BlockSpec(memory_space=pl.ANY),
            scratch_shapes=[pltpu.SemaphoreType.DMA((4,))],
        ),
        input_output_aliases={5: 0} if given else {},
        compiler_params=pltpu.CompilerParams(vmem_limit_bytes=VMEM_LIMIT),
        cost_estimate=pl.CostEstimate(flops=0, bytes_accessed=2 * HEADS * D * D, transcendentals=0),
    )(index, *slots, *given)


def ring_exchange(slots, axis):
    size = lax.axis_size(axis)
    moved = [
        lax.ppermute(slots[d], axis, [(i, (i + d) % size) for i in range(size)]) for d in range(1, len(slots))
    ]
    return [slots[0], *moved]


def swap_rows(array):
    return lax.ppermute(array, "z", [(i, i ^ 1) for i in range(NZ)])


def swap_cores(array):
    return lax.ppermute(array, "core", [(0, 1), (1, 0)])


def local(tokens, queries, keys_in, values, norm_gain, log_decay, doc_ids):
    index = jnp.stack([lax.axis_index(name) for name in ("phase", "y", "core", "z")]).astype(jnp.int32)
    queries, keys, values, decay = queries[0, 0], keys_in[0, 0], values[0, 0], log_decay[0, 0]
    gain = norm_gain.reshape(8, 1, ROWS)

    others_lanes = (1 - index[CORE]) * HALF * D
    others = [lax.dynamic_slice_in_dim(array, others_lanes, HALF * D, 1) for array in (keys, values)]
    other = swap_cores(summaries(True, index, *others, decay, doc_ids))
    own = summaries(False, index, keys, values, decay, doc_ids)

    part, group_states = ((PART, D), BF16), ((ROWS, D), BF16)
    slots = ring_exchange(small_call(chip_kernel, index, [own, other], [part] * 4), "y")
    intra = [intra_term(wave, queries, keys, values, decay, doc_ids) for wave in range(2)]

    pair, pair_states = ((PAIR, D), BF16), ((2 * D, D), BF16)
    send, keep = small_call(
        row_kernel,
        index,
        slots,
        [pair] * 2,
        [pltpu.VMEM((4, PART, D), BF16), pltpu.VMEM((GROUP, D, D), BF16)],
        intra[0][:1],
    )
    partner = swap_rows(send)
    (both,) = small_call(pair_kernel, index, [keep, partner], [pair])
    before = [lax.ppermute(both, "z", [(i, (i + by) % NZ) for i in range(NZ)]) for by in (2, 4, 6)]
    mine, send = small_call(prefix_kernel, index, [keep, partner, *before], [pair_states] * 2)
    spread = small_call(
        spread_kernel,
        index,
        [mine, swap_rows(send), *slots],
        [group_states] * 4,
        [pltpu.VMEM((4, PART, D), BF16), pltpu.VMEM((4, ROWS, D), BF16)],
    )
    spread = ring_exchange(spread, "y")
    for_core = lambda of_other, after: small_call(
        functools.partial(core_kernel, of_other), index, [own, other, *spread], [((4, ROWS, D), BF16)], after=after
    )[0]
    theirs = swap_cores(for_core(True, intra[1][:1]))
    mine = for_core(False, ())

    result = None
    for wave in range(2):
        normed = ring_exchange(attend(wave, index, queries, *intra[wave], mine, theirs, gain), "phase")
        sums = small_call(
            functools.partial(layers_kernel, wave),
            index,
            [tokens[0], *normed],
            [((D, ROWS), BF16)] * 4,
            [pltpu.VMEM((4, D, ROWS), BF16)],
        )
        result = place(wave, index, ring_exchange(sums, "phase"), result)
    return result[None, None]


def solution(mesh):
    grid = Mesh(mesh.devices.reshape(4, NZ, 4, 2), ("phase", "z", "y", "core"))
    ctx = ("z", "y", "core")
    rows = P("phase", None, ctx, None)
    return jax.shard_map(
        local,
        mesh=grid,
        in_specs=(
            P(None, ctx, "phase"),
            rows,
            rows,
            rows,
            P("phase", None),
            P("phase", None, None, ctx),
            P(None, ctx),
        ),
        out_specs=rows,
        check_vma=False,
    )
```
